256 devices in a mesh: dp: 64 (over y, z, core), tensor: 4 (over x).
Axes of the slice: x: 4, y: 4, z: 8, core: 2. Of those that a mesh axis runs over, the one named last changes fastest.
Arguments:
- queries: bfloat16 [2, 512, 8192], P(None, 'dp', 'tensor'), may hold values from -60 to 60
- key_cache: bfloat16 [512, 8, 512, 128], P('dp', 'tensor'), may hold values from -6 to 6
- value_cache: bfloat16 [512, 8, 512, 128], P('dp', 'tensor'), may hold values from -6 to 6
- new_keys: bfloat16 [2, 512, 1024], P(None, 'dp', 'tensor'), may hold values from -8 to 8
- new_values: bfloat16 [2, 512, 1024], P(None, 'dp', 'tensor'), may hold values from -6 to 6
- lengths: int32 [512], P('dp'), may hold values from 64 to 512, as said below
- ancestors: int32 [2, 512], replicated, may hold values from 0 to 511, as said below
- out_weight: bfloat16 [8192, 8192], P('tensor', 'dp'), may hold values from -0.25 to 0.25
Outputs:
- mixed: bfloat16 [2, 512, 8192], P(None, 'tensor', 'dp')
The draws below stay inside these ranges and needn't reach their ends.
Inputs may be any that keep to these rules, and one draw needn't show every extreme that they name: `lengths`: every particle has at least 64 filled slots, and some particle has exactly 512. Each ancestor is a particle of the same prompt: ancestors[r, p] // 32 == p // 32.
All inputs are finite; a program needn't handle non-finite values.
Results may differ from the reference program's by a relative error of at most 0.008.
Values may be sent and summed in bfloat16 or wider, within the bound.
No kernel may reach another device: no remote copies, remote signals or barrier semaphores. Data moves between devices by JAX's collectives and lax.ppermute only.
A program may use at most 64 MiB of HBM per device.

```python
import math
import jax
import jax.numpy as jnp
from jax import lax

D = 8192
HEADS = 64
KV_HEADS = 8
HEAD_DIM = 128
FAMILY = 32
ROUNDS = 2
CACHE = 512
PARTICLES = 512
PROMPTS = 16


def shared_directions(key):
    common_key = jax.random.fold_in(key, 102)
    common = jnp.clip(jax.random.normal(common_key, (KV_HEADS, HEAD_DIM), jnp.float32), -3.0, 3.0)
    return common


def bounded_normal(key, shape):
    return jnp.clip(jax.random.normal(key, shape, jnp.float32), -6.0, 6.0)


def draw_queries(key, part):
    common = shared_directions(key)
    key = jax.random.fold_in(key, 1)
    noise_key = jax.random.fold_in(key, 0)
    shape = (ROUNDS, PARTICLES, HEADS, HEAD_DIM)
    owner = jnp.arange(HEADS) // (HEADS // KV_HEADS)
    lifted = 0.6 * common[owner]
    values = bounded_normal(noise_key, shape) + lifted
    return values.reshape(ROUNDS, PARTICLES, HEADS * HEAD_DIM).astype(jnp.bfloat16)


def draw_key_cache(key, part):
    key = jax.random.fold_in(key, 2)
    shape = (PARTICLES, KV_HEADS, CACHE, HEAD_DIM)
    values = bounded_normal(key, shape)
    return values.astype(jnp.bfloat16)


def draw_new_keys(key, part):
    common = shared_directions(key)
    key = jax.random.fold_in(key, 3)
    shape = (ROUNDS, PARTICLES, KV_HEADS, HEAD_DIM)
    values = bounded_normal(key, shape) + 0.6 * common
    return values.reshape(ROUNDS, PARTICLES, KV_HEADS * HEAD_DIM).astype(jnp.bfloat16)


def draw_lengths(key, part):
    key = jax.random.fold_in(key, 4)
    count_key, spot_key = jax.random.split(key)
    counts = jax.random.randint(count_key, (PARTICLES,), CACHE // 8, CACHE + 1)
    chosen_spot = jax.random.randint(spot_key, (), 0, PARTICLES)
    return jnp.where(jnp.arange(PARTICLES) == chosen_spot, CACHE, counts).astype(jnp.int32)


def draw_ancestors(key, part):
    key = jax.random.fold_in(key, 5)
    order_key, first_key, second_key = jax.random.split(key, 3)
    order_keys = jax.random.split(order_key, ROUNDS * PROMPTS)
    orders = jax.vmap(lambda single: jax.random.permutation(single, FAMILY))(order_keys).reshape(ROUNDS, PROMPTS, FAMILY)
    lanes = jnp.minimum(jax.random.randint(first_key, (ROUNDS, PROMPTS, FAMILY), 0, FAMILY), jax.random.randint(second_key, (ROUNDS, PROMPTS, FAMILY), 0, FAMILY))
    chosen = jnp.take_along_axis(orders, lanes, axis=2)
    return (chosen + jnp.arange(PROMPTS)[None, :, None] * FAMILY).reshape(ROUNDS, PARTICLES).astype(jnp.int32)


def block_levels(stream_key, extent, cuts, smallest, largest):
    gain, own = 1.0, jax.random.fold_in(stream_key, 6)
    for dim, shards_of in cuts:
        steps = jnp.exp(jax.random.uniform(jax.random.fold_in(own, dim), (shards_of,), jnp.float32, smallest / len(cuts), largest / len(cuts)))
        gain = gain * jnp.repeat(steps, extent[dim] // shards_of).reshape([-1 if axis == dim else 1 for axis in range(len(extent))])
    return gain


def noise(key, extent, deviation, most, pieces=(), held_as=jnp.bfloat16):
    loudness = block_levels(key, extent, pieces, -0.22, 0.18) if pieces else 1.0
    values = jax.random.normal(key, extent, jnp.float32) * deviation * loudness
    return jnp.minimum(jnp.maximum(values, -most), most).astype(held_as)


def setup_inputs(seed: int = 0) -> dict:
    seeds = jax.random.split(jax.random.key(seed), 9)
    return {
        "queries": draw_queries(jax.random.fold_in(seeds[8], 71), 0),
        "key_cache": draw_key_cache(jax.random.fold_in(seeds[8], 71), 0),
        "value_cache": noise(seeds[2], (PARTICLES, KV_HEADS, CACHE, HEAD_DIM), 1.0, 6.0, ((0, 64), (1, 4))),
        "new_keys": draw_new_keys(jax.random.fold_in(seeds[8], 71), 0),
        "new_values": noise(seeds[4], (ROUNDS, PARTICLES, KV_HEADS * HEAD_DIM), 1.0, 6.0, ((1, 64), (2, 4))),
        "lengths": draw_lengths(jax.random.fold_in(seeds[8], 71), 0),
        "ancestors": draw_ancestors(jax.random.fold_in(seeds[8], 71), 0),
        "out_weight": noise(seeds[7], (HEADS * HEAD_DIM, D), (HEADS * HEAD_DIM // 16) ** -0.5, 0.25, ((0, 4), (1, 64))),
    }


def reference(queries, key_cache, value_cache, new_keys, new_values, lengths, ancestors, out_weight):
    count_rounds, particles, feature_width = queries.shape
    kv_heads, cache_len, head_dim = key_cache.shape[1:]
    per_group = feature_width // head_dim // kv_heads
    factor = 1.0 / math.sqrt(head_dim)
    lineage = []
    for round_index in range(count_rounds):
        stepped = ancestors[round_index]
        lineage.append(stepped if round_index == 0 else jnp.take(lineage[-1], stepped))
    places = jnp.arange(cache_len, dtype=jnp.int32)
    outputs = []
    for round_index in range(count_rounds):
        roots = lineage[round_index]

        def attend_one(particle, round_index=round_index, roots=roots):
            root_id = roots[particle]
            query_rows = queries[round_index, particle].astype(jnp.float32).reshape(kv_heads, per_group, head_dim)
            key_rows = key_cache[root_id].astype(jnp.float32)
            value_rows = value_cache[root_id].astype(jnp.float32)
            scores = jnp.einsum('gqd,gtd->gqt', query_rows, key_rows) * factor
            inside = places < lengths[root_id]
            summit = lax.optimization_barrier(jnp.max(jnp.where(inside, scores, -jnp.inf), axis=-1))
            weights = jnp.where(inside, jnp.exp(scores - summit[..., None]), 0.0).astype(jnp.bfloat16)
            weights = lax.optimization_barrier(weights).astype(jnp.float32)
            totals = lax.optimization_barrier(jnp.sum(weights, axis=-1))
            mixture = jnp.einsum('gqt,gtd->gqd', weights, value_rows)
            own_key = new_keys[round_index, particle].astype(jnp.float32).reshape(kv_heads, head_dim)
            own_value = new_values[round_index, particle].astype(jnp.float32).reshape(kv_heads, 1, head_dim)
            own_score = jnp.einsum('gqd,gd->gq', query_rows, own_key) * factor
            terms = [(summit, totals, mixture), (own_score, jnp.ones_like(own_score), own_value)]
            if round_index >= 1:
                parent = ancestors[round_index, particle]
                parent_key = new_keys[round_index - 1, parent].astype(jnp.float32).reshape(kv_heads, head_dim)
                parent_value = new_values[round_index - 1, parent].astype(jnp.float32).reshape(kv_heads, 1, head_dim)
                parent_score = jnp.einsum('gqd,gd->gq', query_rows, parent_key) * factor
                terms.append((parent_score, jnp.ones_like(parent_score), parent_value))
            highest = terms[0][0]
            for entry in terms[1:]:
                highest = jnp.maximum(highest, entry[0])
            denominator = jnp.zeros_like(highest)
            numerator = jnp.zeros((kv_heads, per_group, head_dim), jnp.float32)
            for entry in terms:
                scaling = jnp.exp(entry[0] - highest)
                denominator = denominator + entry[1] * scaling
                numerator = numerator + entry[2] * scaling[..., None]
            return (numerator / denominator[..., None]).reshape(feature_width).astype(jnp.bfloat16)
        outputs.append(lax.map(attend_one, jnp.arange(particles, dtype=jnp.int32)))
    attention = jnp.stack(outputs)
    product = jnp.dot(attention.reshape(count_rounds * particles, feature_width), out_weight, preferred_element_type=jnp.float32)
    return product.astype(jnp.bfloat16).reshape(count_rounds, particles, out_weight.shape[1])
```

```python
import math

import jax
import jax.numpy as jnp
from jax import lax
from jax.experimental import pallas as pl
from jax.experimental.pallas import tpu as pltpu
from jax.sharding import Mesh
from jax.sharding import PartitionSpec as P

FAMILY = 32
AXES = ("y", "zo", "zi", "c", "x")
SIZES = (4, 4, 2, 2, 4)
DP = ("y", "zo", "zi", "c")

HOLD = 8
ITEMS = 64
SLOTS = 128
CHUNKS = SLOTS // 8
HEADS = 16
KV = 2
GROUP = 8
HD = 128
FEAT = HEADS * HD
HALF = FEAT // 2
CACHE = 512
NEG = -1e30

VMEM = pl.BlockSpec(memory_space=pltpu.VMEM)
SMEM = pl.BlockSpec(memory_space=pltpu.SMEM)


def plan_kernel(ids_ref, anc_ref, sort_ref, parent_ref, flag_ref, unsort_ref, chunk_ref, count, current):
    first, own, zi, c = ids_ref[0], ids_ref[1], ids_ref[2], ids_ref[3]
    sort_ref[...] = jnp.zeros_like(sort_ref)
    parent_ref[...] = jnp.zeros_like(parent_ref)
    flag_ref[...] = jnp.zeros_like(flag_ref)
    for h in range(HOLD):
        count[h] = 0
        current[h] = 0
    for j in range(CHUNKS + 1):
        chunk_ref[j] = 0
    lane = lax.broadcasted_iota(jnp.int32, (1, 128), 1)

    def step(n, used):
        block, r, i = n // 16, (n // 8) % 2, n % 8
        place = ((zi ^ (block // 2)) * 2 + (c ^ (block % 2))) * 8 + i
        particle = first + place
        mother = anc_ref[1, particle]
        source = jnp.where(r == 1, mother, particle)
        root = anc_ref[0, source] - own
        here = jnp.logical_and(root >= 0, root < HOLD)
        h = jnp.clip(root, 0, HOLD - 1)
        seen = count[h]
        opens = jnp.logical_and(here, seen % 8 == 0)
        chunk = jnp.where(opens, used, current[h])
        current[h] = chunk
        count[h] = seen + jnp.where(here, 1, 0)
        slot = jnp.where(here, chunk * 8 + seen % 8, SLOTS)
        chunk_ref[jnp.where(opens, chunk, CHUNKS)] = h
        sort_ref[pl.ds(slot, 1), :] = jnp.where(lane == n, 1.0, 0.0)
        mp = mother - first
        device = mp // 8
        mblock = ((device // 2) ^ zi) * 2 + ((device % 2) ^ c)
        mn = mblock * 16 + mp % 8
        with_parent = jnp.where(r == 1, 1.0, 0.0)
        parent_ref[pl.ds(slot, 1), :] = jnp.where(lane == mn, 1.0, 0.0) * with_parent
        flag_ref[pl.ds(slot, 1), :] = jnp.zeros((1, 128), jnp.float32) + with_parent
        unsort_ref[pl.ds(r * FAMILY + place, 1), :] = jnp.where(lane == slot, 1.0, 0.0)
        return jnp.where(opens, used + 1, used)

    used = lax.fori_loop(0, ITEMS, step, jnp.int32(0))
    chunk_ref[CHUNKS] = used


def attend_kernel(
    ids_ref,
    chunk_ref,
    len_ref,
    sort_ref,
    parent_ref,
    flag_ref,
    unsort_ref,
    m0,
    m1,
    m2,
    m3,
    key_ref,
    value_ref,
    keep_ref,
    give_ref,
    message,
    ordered,
    mothers,
    answer,
):
    factor = 1.0 / math.sqrt(HD)
    zi, c = ids_ref[2], ids_ref[3]
    for b, m in enumerate((m0, m1, m2, m3)):
        message[b * 16 : b * 16 + 16, :] = m[...]
    sort = sort_ref[0:SLOTS, 0:ITEMS].astype(jnp.bfloat16)
    ordered[...] = jnp.dot(sort, message[...], preferred_element_type=jnp.float32)
    pick = parent_ref[0:SLOTS, 0:ITEMS].astype(jnp.bfloat16)
    mothers[...] = jnp.dot(pick, message[:, FEAT:], preferred_element_type=jnp.float32)
    answer[...] = jnp.zeros_like(answer)
    places = lax.broadcasted_iota(jnp.int32, (1, CACHE), 1)

    def tile(v):
        return jnp.concatenate([v] * GROUP, axis=0)

    def body(j, carry):
        h = chunk_ref[j]
        inside = places < len_ref[h]
        rows = pl.ds(pl.multiple_of(j * 8, 8), 8)
        flag = tile(flag_ref[rows, 0:1]) > 0.5
        for g in range(KV):
            q = jnp.concatenate(
                [ordered[rows, (g * GROUP + k) * HD : (g * GROUP + k + 1) * HD] for k in range(GROUP)], axis=0
            )
            scores = (
                lax.dot_general(
                    q.astype(jnp.bfloat16),
                    key_ref[h, g],
                    (((1,), (1,)), ((), ())),
                    preferred_element_type=jnp.float32,
                )
                * factor
            )
            scores = jnp.where(inside, scores, NEG)
            top = jnp.max(scores, axis=-1, keepdims=True)
            weights = jnp.where(inside, jnp.exp(scores - top), 0.0).astype(jnp.bfloat16)
            mass = jnp.sum(weights.astype(jnp.float32), axis=-1, keepdims=True)
            mix = jnp.dot(weights, value_ref[h, g], preferred_element_type=jnp.float32)
            own_k = tile(ordered[rows, FEAT + g * HD : FEAT + (g + 1) * HD])
            own_v = tile(ordered[rows, FEAT + (KV + g) * HD : FEAT + (KV + g + 1) * HD])
            par_k = tile(mothers[rows, g * HD : (g + 1) * HD])
            par_v = tile(mothers[rows, (KV + g) * HD : (KV + g + 1) * HD])
            own_s = jnp.sum(q * own_k, axis=-1, keepdims=True) * factor
            par_s = jnp.sum(q * par_k, axis=-1, keepdims=True) * factor
            par_s = jnp.where(flag, par_s, NEG)
            peak = jnp.maximum(jnp.maximum(top, own_s), par_s)
            e0 = jnp.exp(top - peak)
            e1 = jnp.exp(own_s - peak)
            e2 = jnp.where(flag, jnp.exp(par_s - peak), 0.0)
            out = (mix * e0 + own_v * e1 + par_v * e2) / (mass * e0 + e1 + e2)
            for k in range(GROUP):
                answer[g, rows, k * HD : (k + 1) * HD] = out[k * 8 : k * 8 + 8]
        return carry

    lax.fori_loop(0, chunk_ref[CHUNKS], body, 0)
    for cc, ref in ((0, keep_ref), (1, give_ref)):
        feats = answer[c ^ cc].astype(jnp.bfloat16)
        for zz in range(2):
            which = pl.ds(pl.multiple_of((zi ^ zz) * FAMILY, FAMILY), FAMILY)
            back = unsort_ref[which, :].astype(jnp.bfloat16)
            ref[zz] = jnp.dot(back, feats, preferred_element_type=jnp.float32).astype(jnp.bfloat16)


def project_kernel(ids_ref, mine_ref, other_ref, w_ref, *outs):
    c, x = ids_ref[3], ids_ref[4]
    lo = pl.ds(pl.multiple_of(c * HALF, HALF), HALF)
    hi = pl.ds(pl.multiple_of((1 - c) * HALF, HALF), HALF)
    for k, out in enumerate(outs):
        y = (x + k) % 4
        total = jnp.dot(mine_ref[...], w_ref[y, lo, :], preferred_element_type=jnp.float32)
        total += jnp.dot(other_ref[...], w_ref[y, hi, :], preferred_element_type=jnp.float32)
        out[...] = total.astype(jnp.bfloat16)


def permute(value, axes, move):
    sizes = [SIZES[AXES.index(a)] for a in axes]
    pairs = []
    total = math.prod(sizes)
    for n in range(total):
        coords, rest = [], n
        for s in reversed(sizes):
            coords.append(rest % s)
            rest //= s
        to = move(*reversed(coords))
        flat = 0
        for t, s in zip(to, sizes):
            flat = flat * s + t % s
        pairs.append((n, flat))
    return lax.ppermute(value, axes, pairs)


def swap_core(v):
    return permute(v, ("c",), lambda c: (1 - c,))


def swap_chip(v):
    return permute(v, ("zi",), lambda z: (1 - z,))


def per_device(queries, key_cache, value_cache, new_keys, new_values, lengths, ancestors, out_weight):
    y, zo, zi, c, x = (lax.axis_index(a) for a in AXES)
    family = y * 4 + zo
    ids = jnp.stack([family * FAMILY, family * FAMILY + (zi * 2 + c) * HOLD, zi, c, x]).astype(jnp.int32)
    weights = lax.all_gather(out_weight, "y", axis=0)
    m0 = jnp.concatenate([queries, new_keys, new_values], axis=-1).reshape(2 * HOLD, FEAT + 2 * KV * HD)
    m2 = swap_chip(m0)
    m1 = swap_core(m0)
    m3 = swap_core(m2)
    f32 = jnp.float32
    sort, parent, flag, unsort, chunk = pl.pallas_call(
        plan_kernel,
        out_shape=[
            jax.ShapeDtypeStruct((SLOTS + 8, 128), f32),
            jax.ShapeDtypeStruct((SLOTS + 8, 128), f32),
            jax.ShapeDtypeStruct((SLOTS + 8, 128), f32),
            jax.ShapeDtypeStruct((ITEMS, 128), f32),
            jax.ShapeDtypeStruct((CHUNKS + 1,), jnp.int32),
        ],
        in_specs=[SMEM, SMEM],
        out_specs=[VMEM, VMEM, VMEM, VMEM, SMEM],
        scratch_shapes=[pltpu.SMEM((HOLD,), jnp.int32), pltpu.SMEM((HOLD,), jnp.int32)],
        name="plan",
    )(ids, ancestors)
    block = jax.ShapeDtypeStruct((2, FAMILY, HALF), jnp.bfloat16)
    keep, give = pl.pallas_call(
        attend_kernel,
        out_shape=[block, block],
        in_specs=[SMEM, SMEM, SMEM] + [VMEM] * 10,
        out_specs=[VMEM, VMEM],
        scratch_shapes=[
            pltpu.VMEM((ITEMS, FEAT + 2 * KV * HD), jnp.bfloat16),
            pltpu.VMEM((SLOTS, FEAT + 2 * KV * HD), f32),
            pltpu.VMEM((SLOTS, 2 * KV * HD), f32),
            pltpu.VMEM((KV, SLOTS, HALF), f32),
        ],
        compiler_params=pltpu.CompilerParams(vmem_limit_bytes=24 * 2**20),
        name="attend",
    )(ids, chunk, lengths, sort, parent, flag, unsort, m0, m1, m2, m3, key_cache, value_cache)
    chip = keep + swap_core(give)
    ours = chip[0] + swap_chip(chip[1])
    gathered = lax.all_gather(ours, ("zi", "zo"), axis=0, tiled=True)
    other = swap_core(gathered)
    rows = gathered.shape[0]
    parts = pl.pallas_call(
        project_kernel,
        out_shape=[jax.ShapeDtypeStruct((rows, 128), jnp.bfloat16)] * 4,
        in_specs=[SMEM, VMEM, VMEM, VMEM],
        out_specs=[VMEM] * 4,
        compiler_params=pltpu.CompilerParams(vmem_limit_bytes=24 * 2**20),
        name="project",
    )(ids, gathered, other, weights)
    total = 0.0
    for k, part in enumerate(parts):
        total = total + permute(part, ("y", "x"), lambda y, x, k=k: (x + k, y)).astype(f32)
    return total.astype(jnp.bfloat16).reshape(2, rows // 2, 128)


def solution(mesh):
    fine = Mesh(mesh.devices.reshape(SIZES), AXES)
    in_specs = (
        P(None, DP, "x"),
        P(DP, "x", None, None),
        P(DP, "x", None, None),
        P(None, DP, "x"),
        P(None, DP, "x"),
        P(DP),
        P(),
        P("x", DP),
    )
    return jax.shard_map(
        per_device, mesh=fine, in_specs=in_specs, out_specs=P(None, "x", DP), check_vma=False
    )
```

```python
import math

import jax
import jax.numpy as jnp
from jax import lax
from jax.experimental import pallas as pl
from jax.experimental.pallas import tpu as pltpu
from jax.sharding import Mesh
from jax.sharding import PartitionSpec as P

FAMILY = 32
AXES = ("y", "zo", "zi", "c", "x")
SIZES = (4, 4, 2, 2, 4)
DP = ("y", "zo", "zi", "c")
Z = ("zo", "zi")

HOLD = 8
ITEMS = 64
CHUNKS = 16
SLOTS = CHUNKS * 8
KV = 2
GROUP = 8
HD = 128
HALF = GROUP * HD
FEAT = KV * HALF
WIDE = FEAT + 2 * KV * HD
CACHE = 512
NEG = -1e30

HBM = pl.BlockSpec(memory_space=pltpu.HBM)
VMEM = pl.BlockSpec(memory_space=pltpu.VMEM)
SMEM = pl.BlockSpec(memory_space=pltpu.SMEM)
F32 = jnp.float32
BF16 = jnp.bfloat16
LIMIT = pltpu.CompilerParams(vmem_limit_bytes=16 * 2**20)
TINY = pl.CostEstimate(flops=10**6, bytes_accessed=10**5, transcendentals=0)


def at(axis):
    return lax.axis_index(axis)


def plan_kernel(
    ancestors, lengths, key_ref, value_ref, w_ref,
    sort_ref, back_ref, chunk_ref, keys, values, w0,
    anc_ref, len_ref, count, current, sems,
):
    loads = [
        pltpu.make_async_copy(src, dst, sems.at[k])
        for k, (src, dst) in enumerate(
            ((ancestors, anc_ref), (lengths, len_ref), (key_ref, keys), (value_ref, values), (w_ref, w0))
        )
    ]
    for load in loads:
        load.start()
    zi, c = at("zi"), at("c")
    first = (at("y") * 4 + at("zo")) * FAMILY
    own = zi * 2 + c
    sort_ref[...] = jnp.zeros_like(sort_ref)
    for h in range(HOLD):
        count[h] = 0
        current[h] = 0
    for j in range(CHUNKS + 2):
        chunk_ref[j] = 0
    for load in loads[:2]:
        load.wait()
    for h in range(HOLD):
        chunk_ref[CHUNKS + 2 + h] = len_ref[h]
    lane = lax.broadcasted_iota(jnp.int32, (1, 128), 1)
    used = jnp.int32(0)
    for n in range(ITEMS):
        block, r, i = n // 16, (n // 8) % 2, n % 8
        place = (lax.bitwise_xor(zi, block // 2) * 2 + lax.bitwise_xor(c, block % 2)) * 8 + i
        particle = first + place
        if r:
            mother = anc_ref[1, particle]
            root = anc_ref[0, mother] - first
            mp = mother - first
            mn = (lax.bitwise_xor(mp >> 4, zi) * 2 + lax.bitwise_xor((mp >> 3) & 1, c)) * 16 + (mp & 7)
        else:
            root = anc_ref[0, particle] - first
        here = (root >> 3) == own
        h = root & 7
        seen = count[h]
        opens = jnp.logical_and(here, (seen & 7) == 0)
        chunk = jnp.where(opens, used, current[h])
        current[h] = chunk
        count[h] = seen + jnp.where(here, 1, 0)
        slot = jnp.where(here, chunk * 8 + (seen & 7), SLOTS)
        chunk_ref[jnp.where(opens, chunk, CHUNKS)] = h
        row = jnp.where(lane == n, 1.0, 0.0)
        if r:
            row = jnp.where(lane == mn + ITEMS, 1.0, row)
        sort_ref[pl.ds(slot, 1), :] = row
        back_ref[pl.ds(r * FAMILY + place, 1), :] = jnp.where(lane == slot, 1.0, 0.0)
        used = jnp.where(opens, used + 1, used)
    chunk_ref[CHUNKS + 1] = used
    for load in loads[2:]:
        load.wait()


def attend_kernel(
    plan, back, chunks, m0, m1, m2, m3, keys, values,
    keep0, keep1, give0, give1,
    message, ordered, mothers, answer,
):
    scale = math.log2(math.e) / math.sqrt(HD)
    zi, c = at("zi"), at("c")
    for b, m in enumerate((m0, m1, m2, m3)):
        message[b * 16 : b * 16 + 16, :] = m[...]
    answer[...] = jnp.zeros_like(answer)
    sort = plan[0:SLOTS, 0:ITEMS].astype(BF16)
    ordered[...] = jnp.dot(sort, message[...], preferred_element_type=F32)
    pick = plan[0:SLOTS, ITEMS : 2 * ITEMS].astype(BF16)
    mothers[...] = jnp.dot(pick, message[:, FEAT:], preferred_element_type=F32)
    places = lax.broadcasted_iota(jnp.int32, (1, CACHE), 1)
    lane = lax.broadcasted_iota(jnp.int32, (8, 128), 1)
    slot = lax.broadcasted_iota(jnp.int32, (8 * GROUP, 128), 0) & 7
    extra = lax.broadcasted_iota(jnp.int32, (8 * GROUP, 128), 1)
    is_own = extra == slot
    is_parent = extra == slot + 8
    blank = jnp.zeros((HD - 16, HD), F32)
    ones = jnp.ones((CACHE + HD, HD), BF16)

    def chunk(j):
        h = chunks[j]
        inside = places < chunks[CHUNKS + 2 + h]
        rows = pl.ds(pl.multiple_of(j * 8, 8), 8)
        has = jnp.sum(jnp.where(lane >= ITEMS, plan[rows, :], 0.0), axis=-1, keepdims=True)
        flag = jnp.concatenate([has] * GROUP, axis=0) > 0.5
        also = jnp.logical_or(is_own, jnp.logical_and(is_parent, flag))
        for g in range(KV):
            lo = g * HALF
            q = jnp.concatenate([ordered[rows, lo + k * HD : lo + (k + 1) * HD] for k in range(GROUP)], axis=0)
            q = q.astype(BF16)
            at_k, at_v = FEAT + g * HD, FEAT + (KV + g) * HD
            new_k = jnp.concatenate([ordered[rows, at_k : at_k + HD], mothers[rows, g * HD : (g + 1) * HD], blank])
            new_v = jnp.concatenate(
                [ordered[rows, at_v : at_v + HD], mothers[rows, (KV + g) * HD : (KV + g + 1) * HD], blank]
            )
            last = (((1,), (1,)), ((), ()))
            scores = lax.dot_general(q, keys[h, g], last, preferred_element_type=F32)
            new_s = lax.dot_general(q, new_k.astype(BF16), last, preferred_element_type=F32)
            scores = jnp.concatenate([jnp.where(inside, scores, NEG), jnp.where(also, new_s, NEG)], axis=1)
            top = jnp.max(scores, axis=-1, keepdims=True)
            weights = jnp.exp2(scores * scale - top * scale).astype(BF16)
            table = jnp.concatenate([values[h, g], new_v.astype(BF16)], axis=0)
            mixed = jnp.dot(weights, jnp.concatenate([table, ones], axis=1), preferred_element_type=F32)
            out = mixed[:, :HD] / mixed[:, HD:]
            for k in range(GROUP):
                answer[g, rows, k * HD : (k + 1) * HD] = out[k * 8 : k * 8 + 8]

    def body(p, carry):
        for u in range(4):
            chunk(4 * p + u)
        return carry

    lax.fori_loop(0, (chunks[CHUNKS + 1] + 3) // 4, body, 0)
    for cc, outs in ((0, (keep0, keep1)), (1, (give0, give1))):
        feats = answer[lax.bitwise_xor(c, cc)].astype(BF16)
        for zz, out in enumerate(outs):
            which = pl.ds(pl.multiple_of(lax.bitwise_xor(zi, zz) * FAMILY, FAMILY), FAMILY)
            out[...] = jnp.dot(back[which, :].astype(BF16), feats, preferred_element_type=F32).astype(BF16)


def halves_kernel(after_ref, w1, w3, lower_ref, upper_ref):
    lower_ref[...] = w1[:HALF]
    upper_ref[...] = w3[HALF:]


def spread_kernel(a_ref, b_ref, c_ref, d_ref, w2a, w2b, out_ref):
    total = (a_ref[...] + b_ref[...]) + (c_ref[...] + d_ref[...])
    for z in range(8):
        out_ref[z] = total


def half_rows(core):
    return pl.ds(pl.multiple_of(core * HALF, HALF), HALF)


def own_half_kernel(mine_ref, w0, w1, w2a, w2b, w3, acc_ref):
    c = at("c")
    rows = half_rows(c)
    for k, w in enumerate((w0[rows, :], w1[rows, :], jnp.where(c == 0, w2a[...], w2b[...]), w3[rows, :])):
        acc_ref[k] = jnp.dot(mine_ref[...], w, preferred_element_type=F32)


def other_half_kernel(other_ref, acc_ref, w0, w1, w2a, w2b, w3, o0, o1, o2, o3):
    c = at("c")
    rows = half_rows(1 - c)
    for k, w in enumerate((w0[rows, :], w1[rows, :], jnp.where(c == 0, w2b[...], w2a[...]), w3[rows, :])):
        total = acc_ref[k] + jnp.dot(other_ref[...], w, preferred_element_type=F32)
        total = total.astype(BF16)
        place = (at("y") - k - at("x")) & 3
        for s, out in enumerate((o0, o1, o2, o3)):

            @pl.when(place == s)
            def _(out=out, total=total):
                for zo in range(4):
                    for zi in range(2):
                        at_row = (zo * 2 + zi) * FAMILY
                        out[zi, zo * FAMILY : (zo + 1) * FAMILY, :] = total[at_row : at_row + FAMILY]


def permute(value, axes, move):
    sizes = [SIZES[AXES.index(a)] for a in axes]
    pairs = []
    for n in range(math.prod(sizes)):
        coords, rest = [], n
        for s in reversed(sizes):
            coords.append(rest % s)
            rest //= s
        flat = 0
        for t, s in zip(move(*reversed(coords)), sizes):
            flat = flat * s + t % s
        pairs.append((n, flat))
    return lax.ppermute(value, axes, pairs)


def swap_core(v):
    return permute(v, ("c",), lambda c: (1 - c,))


def swap_chip(v):
    return permute(v, ("zi",), lambda z: (1 - z,))


def swap_both(v):
    return permute(v, ("zi", "c"), lambda z, c: (1 - z, 1 - c))


def shape(*dims, dtype=BF16):
    return jax.ShapeDtypeStruct(dims, dtype)


def attend_call(*args):
    return pl.pallas_call(
        attend_kernel,
        out_shape=[shape(FAMILY, HALF)] * 4,
        in_specs=[VMEM, VMEM, SMEM] + [VMEM] * 6,
        out_specs=[VMEM] * 4,
        scratch_shapes=[
            pltpu.VMEM((ITEMS, WIDE), BF16),
            pltpu.VMEM((SLOTS, WIDE), F32),
            pltpu.VMEM((SLOTS, 2 * KV * HD), F32),
            pltpu.VMEM((KV, SLOTS, HALF), F32),
        ],
        compiler_params=LIMIT,
        cost_estimate=TINY,
        name="attend",
    )(*args)


def per_device(queries, key_cache, value_cache, new_keys, new_values, lengths, ancestors, out_weight):
    m0 = jnp.concatenate([queries, new_keys, new_values], axis=-1).reshape(2 * HOLD, WIDE)
    m3 = swap_both(m0)
    m2 = swap_chip(m0)
    m1 = swap_core(m0)
    w1 = permute(out_weight, ("y",), lambda y: (y + 1,))
    w3 = permute(out_weight, ("y",), lambda y: (y + 3,))
    sort, back, chunks, keys, values, w0 = pl.pallas_call(
        plan_kernel,
        out_shape=[
            shape(SLOTS + 8, 128, dtype=F32),
            shape(ITEMS, 128, dtype=F32),
            shape(CHUNKS + 2 + HOLD, dtype=jnp.int32),
            pltpu.VMEM(key_cache.shape, BF16),
            pltpu.VMEM(value_cache.shape, BF16),
            pltpu.VMEM(out_weight.shape, BF16),
        ],
        in_specs=[HBM] * 5,
        out_specs=[VMEM, VMEM, SMEM, VMEM, VMEM, VMEM],
        scratch_shapes=[
            pltpu.SMEM(ancestors.shape, jnp.int32),
            pltpu.SMEM((HOLD,), jnp.int32),
            pltpu.SMEM((HOLD,), jnp.int32),
            pltpu.SMEM((HOLD,), jnp.int32),
            pltpu.SemaphoreType.DMA((5,)),
        ],
        compiler_params=LIMIT,
        cost_estimate=TINY,
        name="plan",
    )(*(pltpu.with_memory_space_constraint(v, pltpu.HBM) for v in (ancestors, lengths, key_cache, value_cache, out_weight)))
    keep0, keep1, give0, give1 = attend_call(sort, back, chunks, m0, m1, m2, m3, keys, values)
    half = shape(HALF, 128)
    lower, upper = pl.pallas_call(
        halves_kernel,
        out_shape=[half, half],
        in_specs=[VMEM] * 3,
        out_specs=[VMEM] * 2,
        compiler_params=LIMIT,
        cost_estimate=TINY,
        name="halves",
    )(keep0, w1, w3)
    w2a = permute(lower, ("y",), lambda y: (y + 1,))
    w2b = permute(upper, ("y",), lambda y: (y + 3,))
    far = swap_both(give1)
    near = swap_chip(keep1)
    beside = swap_core(give0)
    spread = pl.pallas_call(
        spread_kernel,
        out_shape=shape(8, FAMILY, HALF),
        in_specs=[VMEM] * 6,
        out_specs=VMEM,
        compiler_params=pltpu.CompilerParams(vmem_limit_bytes=8 * 2**20),
        cost_estimate=pl.CostEstimate(flops=10**5, bytes_accessed=10**5, transcendentals=0),
        name="spread",
    )(keep0, far, near, beside, w2a, w2b)
    mine = lax.all_to_all(spread, Z, split_axis=0, concat_axis=0).reshape(8 * FAMILY, HALF)
    other = swap_core(mine)
    rows = 8 * FAMILY
    w_specs = [VMEM] * 5
    w = (w0, w1, w2a, w2b, w3)
    acc = pl.pallas_call(
        own_half_kernel,
        out_shape=shape(4, rows, 128, dtype=F32),
        in_specs=[VMEM] + w_specs,
        out_specs=VMEM,
        compiler_params=LIMIT,
        cost_estimate=pl.CostEstimate(flops=10**9, bytes_accessed=10**6, transcendentals=0),
        name="own_half",
    )(mine, *w)
    parts = pl.pallas_call(
        other_half_kernel,
        out_shape=[shape(2, rows // 2, 128)] * 4,
        in_specs=[VMEM, VMEM] + w_specs,
        out_specs=[VMEM] * 4,
        compiler_params=LIMIT,
        cost_estimate=pl.CostEstimate(flops=10**9, bytes_accessed=10**6, transcendentals=0),
        name="other_half",
    )(other, acc, *w)
    total = 0.0
    for k in (2, 1, 3, 0):
        total = total + permute(parts[k], ("y", "x"), lambda y, x, k=k: (x + k, y)).astype(F32)
    return total.astype(BF16)


def solution(mesh):
    fine = Mesh(mesh.devices.reshape(SIZES), AXES)
    in_specs = (
        P(None, DP, "x"),
        P(DP, "x", None, None),
        P(DP, "x", None, None),
        P(None, DP, "x"),
        P(None, DP, "x"),
        P(DP),
        P(),
        P("x", DP),
    )
    return jax.shard_map(
        per_device, mesh=fine, in_specs=in_specs, out_specs=P(None, "x", DP), check_vma=False
    )
```

```python
import math

import jax
import jax.numpy as jnp
from jax import lax
from jax.experimental import pallas as pl
from jax.experimental.pallas import tpu as pltpu
from jax.sharding import Mesh
from jax.sharding import PartitionSpec as P

FAMILY = 32
AXES = ("y", "zo", "zi", "c", "x")
SIZES = (4, 4, 2, 2, 4)
DP = ("y", "zo", "zi", "c")
Z = ("zo", "zi")

HOLD = 8
ITEMS = 64
CHUNKS = 16
SLOTS = CHUNKS * 8
KV = 2
GROUP = 8
HD = 128
HALF = GROUP * HD
FEAT = KV * HALF
WIDE = FEAT + 2 * KV * HD
CACHE = 512
NEG = -1e30

HBM = pl.BlockSpec(memory_space=pltpu.HBM)
VMEM = pl.BlockSpec(memory_space=pltpu.VMEM)
SMEM = pl.BlockSpec(memory_space=pltpu.SMEM)
F32 = jnp.float32
BF16 = jnp.bfloat16
LIMIT = pltpu.CompilerParams(vmem_limit_bytes=16 * 2**20)
TINY = pl.CostEstimate(flops=10**6, bytes_accessed=10**5, transcendentals=0)


def at(axis):
    return lax.axis_index(axis)


def plan_kernel(
    ancestors, lengths, key_ref, value_ref, w_ref,
    sort_ref, back_ref, chunk_ref, keys, values, w0,
    anc_ref, len_ref, count, current, sems,
):
    loads = [
        pltpu.make_async_copy(src, dst, sems.at[k])
        for k, (src, dst) in enumerate(
            ((ancestors, anc_ref), (lengths, len_ref), (key_ref, keys), (value_ref, values), (w_ref, w0))
        )
    ]
    for load in loads:
        load.start()
    zi, c = at("zi"), at("c")
    first = (at("y") * 4 + at("zo")) * FAMILY
    own = zi * 2 + c
    sort_ref[...] = jnp.zeros_like(sort_ref)
    for h in range(HOLD):
        count[h] = 0
        current[h] = 0
    for j in range(CHUNKS + 2):
        chunk_ref[j] = 0
    for load in loads[:2]:
        load.wait()
    for h in range(HOLD):
        chunk_ref[CHUNKS + 2 + h] = len_ref[h]
    lane = lax.broadcasted_iota(jnp.int32, (1, 128), 1)
    used = jnp.int32(0)
    for n in range(ITEMS):
        block, r, i = n // 16, (n // 8) % 2, n % 8
        place = (lax.bitwise_xor(zi, block // 2) * 2 + lax.bitwise_xor(c, block % 2)) * 8 + i
        particle = first + place
        if r:
            mother = anc_ref[1, particle]
            root = anc_ref[0, mother] - first
            mp = mother - first
            mn = (lax.bitwise_xor(mp >> 4, zi) * 2 + lax.bitwise_xor((mp >> 3) & 1, c)) * 16 + (mp & 7)
        else:
            root = anc_ref[0, particle] - first
        here = (root >> 3) == own
        h = root & 7
        seen = count[h]
        opens = jnp.logical_and(here, (seen & 7) == 0)
        chunk = jnp.where(opens, used, current[h])
        current[h] = chunk
        count[h] = seen + jnp.where(here, 1, 0)
        slot = jnp.where(here, chunk * 8 + (seen & 7), SLOTS)
        chunk_ref[jnp.where(opens, chunk, CHUNKS)] = h
        row = jnp.where(lane == n, 1.0, 0.0)
        if r:
            row = jnp.where(lane == mn + ITEMS, 1.0, row)
        sort_ref[pl.ds(slot, 1), :] = row
        back_ref[pl.ds(r * FAMILY + place, 1), :] = jnp.where(lane == slot, 1.0, 0.0)
        used = jnp.where(opens, used + 1, used)
    chunk_ref[CHUNKS + 1] = used
    for load in loads[2:]:
        load.wait()


def attend_kernel(
    plan, back, chunks, m0, m1, m2, m3, keys, values,
    keep0, keep1, give0, give1,
    message, ordered, mothers, answer,
):
    scale = math.log2(math.e) / math.sqrt(HD)
    zi, c = at("zi"), at("c")
    for b, m in enumerate((m0, m1, m2, m3)):
        message[b * 16 : b * 16 + 16, :] = m[...]
    answer[...] = jnp.zeros_like(answer)
    sort = plan[0:SLOTS, 0:ITEMS].astype(BF16)
    ordered[...] = jnp.dot(sort, message[...], preferred_element_type=F32)
    pick = plan[0:SLOTS, ITEMS : 2 * ITEMS].astype(BF16)
    mothers[...] = jnp.dot(pick, message[:, FEAT:], preferred_element_type=F32)
    places = lax.broadcasted_iota(jnp.int32, (1, CACHE), 1)
    lane = lax.broadcasted_iota(jnp.int32, (8, 128), 1)
    slot = lax.broadcasted_iota(jnp.int32, (8 * GROUP, 128), 0) & 7
    extra = lax.broadcasted_iota(jnp.int32, (8 * GROUP, 128), 1)
    is_own = extra == slot
    is_parent = extra == slot + 8
    blank = jnp.zeros((HD - 16, HD), F32)
    ones = jnp.ones((CACHE + HD, HD), BF16)

    def chunk(j):
        h = chunks[j]
        inside = places < chunks[CHUNKS + 2 + h]
        rows = pl.ds(pl.multiple_of(j * 8, 8), 8)
        has = jnp.sum(jnp.where(lane >= ITEMS, plan[rows, :], 0.0), axis=-1, keepdims=True)
        flag = jnp.concatenate([has] * GROUP, axis=0) > 0.5
        also = jnp.logical_or(is_own, jnp.logical_and(is_parent, flag))
        for g in range(KV):
            lo = g * HALF
            q = jnp.concatenate([ordered[rows, lo + k * HD : lo + (k + 1) * HD] for k in range(GROUP)], axis=0)
            q = q.astype(BF16)
            at_k, at_v = FEAT + g * HD, FEAT + (KV + g) * HD
            new_k = jnp.concatenate([ordered[rows, at_k : at_k + HD], mothers[rows, g * HD : (g + 1) * HD], blank])
            new_v = jnp.concatenate(
                [ordered[rows, at_v : at_v + HD], mothers[rows, (KV + g) * HD : (KV + g + 1) * HD], blank]
            )
            last = (((1,), (1,)), ((), ()))
            scores = lax.dot_general(q, keys[h, g], last, preferred_element_type=F32)
            new_s = lax.dot_general(q, new_k.astype(BF16), last, preferred_element_type=F32)
            scores = jnp.concatenate([jnp.where(inside, scores, NEG), jnp.where(also, new_s, NEG)], axis=1)
            top = jnp.max(scores, axis=-1, keepdims=True)
            weights = jnp.exp2(scores * scale - top * scale).astype(BF16)
            table = jnp.concatenate([values[h, g], new_v.astype(BF16)], axis=0)
            mixed = jnp.dot(weights, jnp.concatenate([table, ones], axis=1), preferred_element_type=F32)
            out = mixed[:, :HD] / mixed[:, HD:]
            for k in range(GROUP):
                answer[g, rows, k * HD : (k + 1) * HD] = out[k * 8 : k * 8 + 8]

    def body(p, carry):
        for u in range(4):
            chunk(4 * p + u)
        return carry

    lax.fori_loop(0, (chunks[CHUNKS + 1] + 3) // 4, body, 0)
    for cc, outs in ((0, (keep0, keep1)), (1, (give0, give1))):
        feats = answer[lax.bitwise_xor(c, cc)].astype(BF16)
        for zz, out in enumerate(outs):
            which = pl.ds(pl.multiple_of(lax.bitwise_xor(zi, zz) * FAMILY, FAMILY), FAMILY)
            out[...] = jnp.dot(back[which, :].astype(BF16), feats, preferred_element_type=F32).astype(BF16)


def halves_kernel(w1, w3, lower_ref, upper_ref):
    lower_ref[...] = w1[:HALF]
    upper_ref[...] = w3[HALF:]


def spread_kernel(a_ref, b_ref, c_ref, d_ref, w1, w3, out_ref):
    total = (a_ref[...] + b_ref[...]) + (c_ref[...] + d_ref[...])
    for z in range(8):
        out_ref[z] = total


def hold_kernel(mine_ref, w2a, w2b, out_ref):
    pass


def half_rows(core):
    return pl.ds(pl.multiple_of(core * HALF, HALF), HALF)


def own_half_kernel(mine_ref, w0, w1, w2a, w2b, w3, acc_ref):
    c = at("c")
    rows = half_rows(c)
    for k, w in enumerate((w0[rows, :], w1[rows, :], jnp.where(c == 0, w2a[...], w2b[...]), w3[rows, :])):
        acc_ref[k] = jnp.dot(mine_ref[...], w, preferred_element_type=F32)


def other_half_kernel(other_ref, acc_ref, w0, w1, w2a, w2b, w3, o0, o1, o2, o3, blocks):
    c = at("c")
    rows = half_rows(1 - c)
    for k, w in enumerate((w0[rows, :], w1[rows, :], jnp.where(c == 0, w2b[...], w2a[...]), w3[rows, :])):
        total = acc_ref[k] + jnp.dot(other_ref[...], w, preferred_element_type=F32)
        total = total.astype(BF16)
        for zo in range(4):
            for zi in range(2):
                at_row = (zo * 2 + zi) * FAMILY
                blocks[k, zi, zo * FAMILY : (zo + 1) * FAMILY, :] = total[at_row : at_row + FAMILY]
    for s, out in enumerate((o0, o1, o2, o3)):
        out[...] = blocks[(at("y") - at("x") - s) & 3]


def permute(value, axes, move):
    sizes = [SIZES[AXES.index(a)] for a in axes]
    pairs = []
    for n in range(math.prod(sizes)):
        coords, rest = [], n
        for s in reversed(sizes):
            coords.append(rest % s)
            rest //= s
        flat = 0
        for t, s in zip(move(*reversed(coords)), sizes):
            flat = flat * s + t % s
        pairs.append((n, flat))
    return lax.ppermute(value, axes, pairs)


def swap_core(v):
    return permute(v, ("c",), lambda c: (1 - c,))


def swap_chip(v):
    return permute(v, ("zi",), lambda z: (1 - z,))


def swap_both(v):
    return permute(v, ("zi", "c"), lambda z, c: (1 - z, 1 - c))


def shape(*dims, dtype=BF16):
    return jax.ShapeDtypeStruct(dims, dtype)


def attend_call(*args):
    return pl.pallas_call(
        attend_kernel,
        out_shape=[shape(FAMILY, HALF)] * 4,
        in_specs=[VMEM, VMEM, SMEM] + [VMEM] * 6,
        out_specs=[VMEM] * 4,
        scratch_shapes=[
            pltpu.VMEM((ITEMS, WIDE), BF16),
            pltpu.VMEM((SLOTS, WIDE), F32),
            pltpu.VMEM((SLOTS, 2 * KV * HD), F32),
            pltpu.VMEM((KV, SLOTS, HALF), F32),
        ],
        compiler_params=LIMIT,
        cost_estimate=TINY,
        name="attend",
    )(*args)


def per_device(queries, key_cache, value_cache, new_keys, new_values, lengths, ancestors, out_weight):
    m0 = jnp.concatenate([queries, new_keys, new_values], axis=-1).reshape(2 * HOLD, WIDE)
    m1 = swap_core(m0)
    m2 = swap_chip(m0)
    m3 = swap_both(m0)
    w1 = permute(out_weight, ("y",), lambda y: (y + 1,))
    w3 = permute(out_weight, ("y",), lambda y: (y + 3,))
    sort, back, chunks, keys, values, w0 = pl.pallas_call(
        plan_kernel,
        out_shape=[
            shape(SLOTS + 8, 128, dtype=F32),
            shape(ITEMS, 128, dtype=F32),
            shape(CHUNKS + 2 + HOLD, dtype=jnp.int32),
            pltpu.VMEM(key_cache.shape, BF16),
            pltpu.VMEM(value_cache.shape, BF16),
            pltpu.VMEM(out_weight.shape, BF16),
        ],
        in_specs=[HBM] * 5,
        out_specs=[VMEM, VMEM, SMEM, VMEM, VMEM, VMEM],
        scratch_shapes=[
            pltpu.SMEM(ancestors.shape, jnp.int32),
            pltpu.SMEM((HOLD,), jnp.int32),
            pltpu.SMEM((HOLD,), jnp.int32),
            pltpu.SMEM((HOLD,), jnp.int32),
            pltpu.SemaphoreType.DMA((5,)),
        ],
        compiler_params=LIMIT,
        cost_estimate=TINY,
        name="plan",
    )(*(pltpu.with_memory_space_constraint(v, pltpu.HBM) for v in (ancestors, lengths, key_cache, value_cache, out_weight)))
    keep0, keep1, give0, give1 = attend_call(sort, back, chunks, m0, m1, m2, m3, keys, values)
    half = shape(HALF, 128)
    lower, upper = pl.pallas_call(
        halves_kernel,
        out_shape=[half, half],
        in_specs=[VMEM] * 2,
        out_specs=[VMEM] * 2,
        compiler_params=LIMIT,
        cost_estimate=TINY,
        name="halves",
    )(w1, w3)
    w2a = permute(lower, ("y",), lambda y: (y + 1,))
    w2b = permute(upper, ("y",), lambda y: (y + 3,))
    far = swap_both(give1)
    near = swap_chip(keep1)
    beside = swap_core(give0)
    spread = pl.pallas_call(
        spread_kernel,
        out_shape=shape(8, FAMILY, HALF),
        in_specs=[VMEM] * 6,
        out_specs=VMEM,
        compiler_params=pltpu.CompilerParams(vmem_limit_bytes=8 * 2**20),
        cost_estimate=pl.CostEstimate(flops=10**5, bytes_accessed=10**5, transcendentals=0),
        name="spread",
    )(keep0, far, near, beside, w1, w3)
    mine = lax.all_to_all(spread, Z, split_axis=0, concat_axis=0).reshape(8 * FAMILY, HALF)
    rows = 8 * FAMILY
    w_specs = [VMEM] * 5
    w = (w0, w1, w2a, w2b, w3)
    mine = pl.pallas_call(
        hold_kernel,
        out_shape=shape(8 * FAMILY, HALF),
        in_specs=[VMEM] * 3,
        out_specs=VMEM,
        input_output_aliases={0: 0},
        compiler_params=LIMIT,
        cost_estimate=TINY,
        name="hold",
    )(mine, w2a, w2b)
    other = swap_core(mine)
    acc = pl.pallas_call(
        own_half_kernel,
        out_shape=shape(4, rows, 128, dtype=F32),
        in_specs=[VMEM] + w_specs,
        out_specs=VMEM,
        compiler_params=LIMIT,
        cost_estimate=pl.CostEstimate(flops=10**9, bytes_accessed=10**6, transcendentals=0),
        name="own_half",
    )(mine, *w)
    parts = pl.pallas_call(
        other_half_kernel,
        out_shape=[shape(2, rows // 2, 128)] * 4,
        in_specs=[VMEM, VMEM] + w_specs,
        out_specs=[VMEM] * 4,
        scratch_shapes=[pltpu.VMEM((4, 2, rows // 2, 128), BF16)],
        compiler_params=LIMIT,
        cost_estimate=pl.CostEstimate(flops=10**9, bytes_accessed=10**6, transcendentals=0),
        name="other_half",
    )(other, acc, *w)
    total = 0.0
    for k in (2, 1, 3, 0):
        total = total + permute(parts[k], ("y", "x"), lambda y, x, k=k: (x + k, y)).astype(F32)
    return total.astype(BF16)


def solution(mesh):
    fine = Mesh(mesh.devices.reshape(SIZES), AXES)
    in_specs = (
        P(None, DP, "x"),
        P(DP, "x", None, None),
        P(DP, "x", None, None),
        P(None, DP, "x"),
        P(None, DP, "x"),
        P(DP),
        P(),
        P("x", DP),
    )
    return jax.shard_map(
        per_device, mesh=fine, in_specs=in_specs, out_specs=P(None, "x", DP), check_vma=False
    )
```

```python
import math

import jax
import jax.numpy as jnp
from jax import lax
from jax.experimental import pallas as pl
from jax.experimental.pallas import tpu as pltpu
from jax.sharding import Mesh
from jax.sharding import PartitionSpec as P

FAMILY = 32
AXES = ("y", "zo", "zi", "c", "x")
SIZES = (4, 4, 2, 2, 4)
DP = ("y", "zo", "zi", "c")
Z = ("zo", "zi")

HOLD = 8
ITEMS = 64
CHUNKS = 16
SLOTS = CHUNKS * 8
KV = 2
GROUP = 8
HD = 128
HALF = GROUP * HD
FEAT = KV * HALF
WIDE = FEAT + 2 * KV * HD
CACHE = 512
NEG = -1e30

HBM = pl.BlockSpec(memory_space=pltpu.HBM)
VMEM = pl.BlockSpec(memory_space=pltpu.VMEM)
SMEM = pl.BlockSpec(memory_space=pltpu.SMEM)
F32 = jnp.float32
BF16 = jnp.bfloat16
LIMIT = pltpu.CompilerParams(vmem_limit_bytes=16 * 2**20)
TINY = pl.CostEstimate(flops=10**6, bytes_accessed=10**5, transcendentals=0)


def at(axis):
    return lax.axis_index(axis)


def plan_kernel(
    ancestors, lengths, key_ref, value_ref, w_ref,
    sort_ref, back_ref, chunk_ref, keys, values, w0,
    anc_ref, len_ref, free, sems,
):
    loads = [
        pltpu.make_async_copy(src, dst, sems.at[k])
        for k, (src, dst) in enumerate(
            ((ancestors, anc_ref), (lengths, len_ref), (key_ref, keys), (value_ref, values), (w_ref, w0))
        )
    ]
    for load in loads:
        load.start()
    first = (at("y") * 4 + at("zo")) * FAMILY
    own = at("zi") * 2 + at("c")
    sort_ref[...] = jnp.zeros_like(sort_ref)
    for j in range(CHUNKS + 2):
        chunk_ref[j] = 0
    for h in range(HOLD):
        free[h] = 0
    free[HOLD] = SLOTS + 1
    lane = lax.broadcasted_iota(jnp.int32, (1, 128), 1)
    used = jnp.int32(0)
    for load in loads[:2]:
        load.wait()
    for h in range(HOLD):
        chunk_ref[CHUNKS + 2 + h] = len_ref[h]
    for block in range(4):
        place = lax.bitwise_xor(own, block) * 8
        for r in range(2):
            for i in range(8):
                n = block * 16 + r * 8 + i
                row = lane == n
                source = first + place + i
                if r:
                    source = anc_ref[1, source]
                    mp = source - first
                    row = jnp.logical_or(row, lane == lax.bitwise_xor(mp >> 3, own) * 16 + (mp & 7) + ITEMS)
                root = anc_ref[0, source] - first
                here = (root >> 3) == own
                h = jnp.where(here, root & 7, HOLD)
                slot = free[h]
                opens = (slot & 7) == 0
                slot = jnp.where(opens, used * 8, slot)
                free[h] = slot + jnp.where(here, 1, 0)
                chunk_ref[jnp.where(opens, used, CHUNKS)] = h
                used = used + jnp.where(opens, 1, 0)
                sort_ref[pl.ds(slot, 1), :] = jnp.where(row, 1.0, 0.0)
                back_ref[pl.ds(r * FAMILY + place + i, 1), :] = jnp.where(lane == slot, 1.0, 0.0)
    chunk_ref[CHUNKS + 1] = used
    for load in loads[2:]:
        load.wait()


def attend_kernel(
    plan, back, chunks, m0, m1, m2, m3, keys, values,
    keep0, keep1, give0, give1,
    message, ordered, mothers, answer,
):
    scale = math.log2(math.e) / math.sqrt(HD)
    zi, c = at("zi"), at("c")
    for b, m in enumerate((m0, m1, m2, m3)):
        message[b * 16 : b * 16 + 16, :] = m[...]
    answer[...] = jnp.zeros_like(answer)
    sort = plan[0:SLOTS, 0:ITEMS].astype(BF16)
    ordered[...] = jnp.dot(sort, message[...], preferred_element_type=F32)
    pick = plan[0:SLOTS, ITEMS : 2 * ITEMS].astype(BF16)
    mothers[...] = jnp.dot(pick, message[:, FEAT:], preferred_element_type=F32)
    places = lax.broadcasted_iota(jnp.int32, (1, CACHE), 1)
    lane = lax.broadcasted_iota(jnp.int32, (8, 128), 1)
    slot = lax.broadcasted_iota(jnp.int32, (8 * GROUP, 128), 0) & 7
    extra = lax.broadcasted_iota(jnp.int32, (8 * GROUP, 128), 1)
    ones = jnp.ones((HD, HD), BF16)
    last = (((1,), (1,)), ((), ()))

    def body(p, carry):
        jobs = []
        for u in range(4):
            j = 4 * p + u
            h = chunks[j]
            inside = places < chunks[CHUNKS + 2 + h]
            rows = pl.ds(pl.multiple_of(j * 8, 8), 8)
            has = jnp.sum(jnp.where(lane >= ITEMS, plan[rows, :], 0.0), axis=-1, keepdims=True)
            flag = jnp.concatenate([has] * GROUP, axis=0) > 0.5
            for g in range(KV):
                lo = g * HALF
                q = jnp.concatenate([ordered[rows, lo + k * HD : lo + (k + 1) * HD] for k in range(GROUP)], axis=0)
                at_k, at_v = FEAT + g * HD, FEAT + (KV + g) * HD
                new_k = [ordered[rows, at_k : at_k + HD], mothers[rows, g * HD : (g + 1) * HD]]
                new_v = [ordered[rows, at_v : at_v + HD], mothers[rows, (KV + g) * HD : (KV + g + 1) * HD]]
                base = 16 * len(jobs)
                also = jnp.logical_or(extra == slot + base, jnp.logical_and(extra == slot + base + 8, flag))
                jobs.append((h, g, rows, inside, also, q.astype(BF16), new_k, new_v))
        new_k = jnp.concatenate([v for job in jobs for v in job[6]]).astype(BF16)
        new_v = jnp.concatenate([v for job in jobs for v in job[7]]).astype(BF16)
        new_s = lax.dot_general(
            jnp.concatenate([job[5] for job in jobs]), new_k, last, preferred_element_type=F32
        )
        mixes, new_w, folded, rest = [], [], [], []
        for w, (h, g, rows, inside, also, q, _, _) in enumerate(jobs):
            scores = lax.dot_general(q, keys[h, g], last, preferred_element_type=F32)
            fresh = new_s[w * 8 * GROUP : (w + 1) * 8 * GROUP]
            scores = jnp.concatenate([jnp.where(inside, scores, NEG), jnp.where(also, fresh, NEG)], axis=1)
            top = jnp.max(scores, axis=-1, keepdims=True)
            weights = jnp.exp2(scores * scale - top * scale).astype(BF16)
            parts = [weights[:, n * 128 : (n + 1) * 128].astype(F32) for n in range(5)]
            total = ((parts[0] + parts[1]) + (parts[2] + parts[3])) + parts[4]
            folded.append(total.astype(BF16))
            rest.append((total - folded[-1].astype(F32)).astype(BF16))
            mixes.append(jnp.dot(weights[:, :CACHE], values[h, g], preferred_element_type=F32))
            new_w.append(weights[:, CACHE:])
        new_mix = jnp.dot(jnp.concatenate(new_w), new_v, preferred_element_type=F32)
        mass = jnp.dot(jnp.concatenate(folded), ones, preferred_element_type=F32)
        mass += jnp.dot(jnp.concatenate(rest), ones, preferred_element_type=F32)
        for w, (h, g, rows, _, _, _, _, _) in enumerate(jobs):
            mine = slice(w * 8 * GROUP, (w + 1) * 8 * GROUP)
            out = (mixes[w] + new_mix[mine]) / mass[mine]
            for k in range(GROUP):
                answer[g, rows, k * HD : (k + 1) * HD] = out[k * 8 : k * 8 + 8]
        return carry

    lax.fori_loop(0, (chunks[CHUNKS + 1] + 3) // 4, body, 0)
    which = [pl.ds(pl.multiple_of(lax.bitwise_xor(zi, zz) * FAMILY, FAMILY), FAMILY) for zz in range(2)]
    turn = jnp.concatenate([back[w, :] for w in which]).astype(BF16)
    for cc, outs in ((0, (keep0, keep1)), (1, (give0, give1))):
        feats = answer[lax.bitwise_xor(c, cc)].astype(BF16)
        both = jnp.dot(turn, feats, preferred_element_type=F32).astype(BF16)
        for zz, out in enumerate(outs):
            out[...] = both[zz * FAMILY : (zz + 1) * FAMILY]


def spread_kernel(a_ref, b_ref, c_ref, d_ref, w1, w3, out_ref):
    total = (a_ref[...] + b_ref[...]) + (c_ref[...] + d_ref[...])
    for z in range(8):
        out_ref[z] = total


def hold_kernel(*refs):
    pass


def half_rows(core):
    return pl.ds(pl.multiple_of(core * HALF, HALF), HALF)


def own_half_kernel(mine_ref, w0, w1, w2, w3, acc_ref):
    rows = half_rows(at("c"))
    for k, w in enumerate((w0, w1, w2, w3)):
        acc_ref[k] = jnp.dot(mine_ref[...], w[rows, :], preferred_element_type=F32)


def other_half_kernel(other_ref, acc_ref, w0, w1, w2, w3, o0, o1, o2, o3, blocks):
    c = at("c")
    rows = half_rows(1 - c)
    for k, w in enumerate((w0, w1, w2, w3)):
        total = acc_ref[k] + jnp.dot(other_ref[...], w[rows, :], preferred_element_type=F32)
        total = total.astype(BF16)
        where = jnp.where(c == 0, k, (4 - k) & 3)
        for zo in range(4):
            for zi in range(2):
                at_row = (zo * 2 + zi) * FAMILY
                blocks[where, zi, zo * FAMILY : (zo + 1) * FAMILY, :] = total[at_row : at_row + FAMILY]
    for s, out in enumerate((o0, o1, o2, o3)):
        out[...] = blocks[(at("y") - at("x") - s) & 3]


def permute(value, axes, move):
    sizes = [SIZES[AXES.index(a)] for a in axes]
    pairs = []
    for n in range(math.prod(sizes)):
        coords, rest = [], n
        for s in reversed(sizes):
            coords.append(rest % s)
            rest //= s
        flat = 0
        for t, s in zip(move(*reversed(coords)), sizes):
            flat = flat * s + t % s
        pairs.append((n, flat))
    return lax.ppermute(value, axes, pairs)


def swap_core(v):
    return permute(v, ("c",), lambda c: (1 - c,))


def swap_chip(v):
    return permute(v, ("zi",), lambda z: (1 - z,))


def swap_both(v):
    return permute(v, ("zi", "c"), lambda z, c: (1 - z, 1 - c))


def shape(*dims, dtype=BF16):
    return jax.ShapeDtypeStruct(dims, dtype)


def attend_call(*args):
    return pl.pallas_call(
        attend_kernel,
        out_shape=[shape(FAMILY, HALF)] * 4,
        in_specs=[VMEM, VMEM, SMEM] + [VMEM] * 6,
        out_specs=[VMEM] * 4,
        scratch_shapes=[
            pltpu.VMEM((ITEMS, WIDE), BF16),
            pltpu.VMEM((SLOTS, WIDE), F32),
            pltpu.VMEM((SLOTS, 2 * KV * HD), F32),
            pltpu.VMEM((KV, SLOTS, HALF), F32),
        ],
        compiler_params=LIMIT,
        cost_estimate=TINY,
        name="attend",
    )(*args)


def per_device(queries, key_cache, value_cache, new_keys, new_values, lengths, ancestors, out_weight):
    m0 = jnp.concatenate([queries, new_keys, new_values], axis=-1).reshape(2 * HOLD, WIDE)
    m1 = swap_core(m0)
    m2 = swap_chip(m0)
    sort, back, chunks, keys, values, w0 = pl.pallas_call(
        plan_kernel,
        out_shape=[
            shape(SLOTS + 8, 128, dtype=F32),
            shape(ITEMS, 128, dtype=F32),
            shape(CHUNKS + 2 + HOLD, dtype=jnp.int32),
            pltpu.VMEM(key_cache.shape, BF16),
            pltpu.VMEM(value_cache.shape, BF16),
            pltpu.VMEM(out_weight.shape, BF16),
        ],
        in_specs=[HBM] * 5,
        out_specs=[VMEM, VMEM, SMEM, VMEM, VMEM, VMEM],
        scratch_shapes=[
            pltpu.SMEM(ancestors.shape, jnp.int32),
            pltpu.SMEM((HOLD,), jnp.int32),
            pltpu.SMEM((HOLD + 1,), jnp.int32),
            pltpu.SemaphoreType.DMA((5,)),
        ],
        compiler_params=LIMIT,
        cost_estimate=TINY,
        name="plan",
    )(*(pltpu.with_memory_space_constraint(v, pltpu.HBM) for v in (ancestors, lengths, key_cache, value_cache, out_weight)))
    def along(v):
        return permute(v, ("y", "c"), lambda y, c: (y + 1 + 2 * c, c))

    w_next = along(out_weight)
    w0_x = swap_core(out_weight)
    w_far = along(w_next)
    w_back = swap_core(along(w0_x))

    m2 = pl.pallas_call(
        hold_kernel,
        out_shape=shape(2 * HOLD, WIDE),
        in_specs=[VMEM] * 2,
        out_specs=VMEM,
        input_output_aliases={0: 0},
        compiler_params=LIMIT,
        cost_estimate=TINY,
        name="relay",
    )(m2, back)
    m3 = swap_core(m2)
    keep0, keep1, give0, give1 = attend_call(sort, back, chunks, m0, m1, m2, m3, keys, values)
    far = swap_both(give1)
    near = swap_chip(keep1)
    beside = swap_core(give0)
    spread = pl.pallas_call(
        spread_kernel,
        out_shape=shape(8, FAMILY, HALF),
        in_specs=[VMEM] * 6,
        out_specs=VMEM,
        compiler_params=pltpu.CompilerParams(vmem_limit_bytes=8 * 2**20),
        cost_estimate=pl.CostEstimate(flops=10**5, bytes_accessed=10**5, transcendentals=0),
        name="spread",
    )(keep0, far, near, beside, w_next, w0_x)
    mine = lax.all_to_all(spread, Z, split_axis=0, concat_axis=0).reshape(8 * FAMILY, HALF)
    rows = 8 * FAMILY
    w_specs = [VMEM] * 4
    w = (w0, w_next, w_far, w_back)
    mine = pl.pallas_call(
        hold_kernel,
        out_shape=shape(8 * FAMILY, HALF),
        in_specs=[VMEM] * 3,
        out_specs=VMEM,
        input_output_aliases={0: 0},
        compiler_params=LIMIT,
        cost_estimate=TINY,
        name="hold",
    )(mine, w_far, w_back)
    other = swap_core(mine)
    acc = pl.pallas_call(
        own_half_kernel,
        out_shape=shape(4, rows, 128, dtype=F32),
        in_specs=[VMEM] + w_specs,
        out_specs=VMEM,
        compiler_params=LIMIT,
        cost_estimate=pl.CostEstimate(flops=10**9, bytes_accessed=10**6, transcendentals=0),
        name="own_half",
    )(mine, *w)
    parts = pl.pallas_call(
        other_half_kernel,
        out_shape=[shape(2, rows // 2, 128)] * 4,
        in_specs=[VMEM, VMEM] + w_specs,
        out_specs=[VMEM] * 4,
        scratch_shapes=[pltpu.VMEM((4, 2, rows // 2, 128), BF16)],
        compiler_params=LIMIT,
        cost_estimate=pl.CostEstimate(flops=10**9, bytes_accessed=10**6, transcendentals=0),
        name="other_half",
    )(other, acc, *w)
    total = 0.0
    for k in (2, 1, 3, 0):
        total = total + permute(parts[k], ("y", "x"), lambda y, x, k=k: (x + k, y)).astype(F32)
    return total.astype(BF16)


def solution(mesh):
    fine = Mesh(mesh.devices.reshape(SIZES), AXES)
    in_specs = (
        P(None, DP, "x"),
        P(DP, "x", None, None),
        P(DP, "x", None, None),
        P(None, DP, "x"),
        P(None, DP, "x"),
        P(DP),
        P(),
        P("x", DP),
    )
    return jax.shard_map(
        per_device, mesh=fine, in_specs=in_specs, out_specs=P(None, "x", DP), check_vma=False
    )
```

```python
import math

import jax
import jax.numpy as jnp
from jax import lax
from jax.experimental import pallas as pl
from jax.experimental.pallas import tpu as pltpu
from jax.sharding import Mesh
from jax.sharding import PartitionSpec as P

FAMILY = 32
AXES = ("y", "zo", "zi", "c", "x")
SIZES = (4, 4, 2, 2, 4)
DP = ("y", "zo", "zi", "c")
Z = ("zo", "zi")

HOLD = 8
ITEMS = 64
CHUNKS = 16
SLOTS = CHUNKS * 8
KV = 2
GROUP = 8
HD = 128
HALF = GROUP * HD
FEAT = KV * HALF
WIDE = FEAT + 2 * KV * HD
CACHE = 512
NEG = -1e30

HBM = pl.BlockSpec(memory_space=pltpu.HBM)
VMEM = pl.BlockSpec(memory_space=pltpu.VMEM)
SMEM = pl.BlockSpec(memory_space=pltpu.SMEM)
F32 = jnp.float32
BF16 = jnp.bfloat16
LIMIT = pltpu.CompilerParams(vmem_limit_bytes=16 * 2**20)
TINY = pl.CostEstimate(flops=10**6, bytes_accessed=10**5, transcendentals=0)


def at(axis):
    return lax.axis_index(axis)


def plan_kernel(
    ancestors, lengths, key_ref, value_ref, w_ref,
    sort_ref, back_ref, chunk_ref, keys, values, w0,
    anc_ref, len_ref, free, sems,
):
    loads = [
        pltpu.make_async_copy(src, dst, sems.at[k])
        for k, (src, dst) in enumerate(
            ((ancestors, anc_ref), (lengths, len_ref), (key_ref, keys), (value_ref, values), (w_ref, w0))
        )
    ]
    for load in loads:
        load.start()
    first = (at("y") * 4 + at("zo")) * FAMILY
    own = at("zi") * 2 + at("c")
    sort_ref[...] = jnp.zeros_like(sort_ref)
    for j in range(CHUNKS + 2):
        chunk_ref[j] = 0
    for h in range(HOLD):
        free[h] = 0
    free[HOLD] = SLOTS + 1
    lane = lax.broadcasted_iota(jnp.int32, (1, 128), 1)
    used = jnp.int32(0)
    for load in loads[:2]:
        load.wait()
    for h in range(HOLD):
        chunk_ref[CHUNKS + 2 + h] = len_ref[h]
    for block in range(4):
        place = lax.bitwise_xor(own, block) * 8
        for r in range(2):
            for i in range(8):
                n = block * 16 + r * 8 + i
                row = lane == n
                source = first + place + i
                if r:
                    source = anc_ref[1, source]
                    mp = source - first
                    row = jnp.logical_or(row, lane == lax.bitwise_xor(mp >> 3, own) * 16 + (mp & 7) + ITEMS)
                root = anc_ref[0, source] - first
                here = (root >> 3) == own
                h = jnp.where(here, root & 7, HOLD)
                slot = free[h]
                opens = (slot & 7) == 0
                slot = jnp.where(opens, used * 8, slot)
                free[h] = slot + jnp.where(here, 1, 0)
                chunk_ref[jnp.where(opens, used, CHUNKS)] = h
                used = used + jnp.where(opens, 1, 0)
                sort_ref[pl.ds(slot, 1), :] = jnp.where(row, 1.0, 0.0)
                back_ref[pl.ds(r * FAMILY + place + i, 1), :] = jnp.where(lane == slot, 1.0, 0.0)
    chunk_ref[CHUNKS + 1] = used
    for load in loads[2:]:
        load.wait()


def attend_kernel(
    plan, back, chunks, m0, m1, m2, m3, keys, values,
    keep0, keep1, give0, give1,
    message, ordered, mothers, answer,
):
    scale = math.log2(math.e) / math.sqrt(HD)
    zi, c = at("zi"), at("c")
    for b, m in enumerate((m0, m1, m2, m3)):
        message[b * 16 : b * 16 + 16, :] = m[...]
    answer[...] = jnp.zeros_like(answer)
    sort = plan[0:SLOTS, 0:ITEMS].astype(BF16)
    ordered[...] = jnp.dot(sort, message[...], preferred_element_type=F32)
    pick = plan[0:SLOTS, ITEMS : 2 * ITEMS].astype(BF16)
    mothers[...] = jnp.dot(pick, message[:, FEAT:], preferred_element_type=F32)
    places = lax.broadcasted_iota(jnp.int32, (1, CACHE), 1)
    lane = lax.broadcasted_iota(jnp.int32, (8, 128), 1)
    slot = lax.broadcasted_iota(jnp.int32, (8 * GROUP, 128), 0) & 7
    extra = lax.broadcasted_iota(jnp.int32, (8 * GROUP, 128), 1)
    ones = jnp.ones((HD, HD), BF16)
    last = (((1,), (1,)), ((), ()))

    def body(p, carry):
        jobs = []
        for u in range(4):
            j = 4 * p + u
            h = chunks[j]
            inside = places < chunks[CHUNKS + 2 + h]
            rows = pl.ds(pl.multiple_of(j * 8, 8), 8)
            has = jnp.sum(jnp.where(lane >= ITEMS, plan[rows, :], 0.0), axis=-1, keepdims=True)
            flag = jnp.concatenate([has] * GROUP, axis=0) > 0.5
            for g in range(KV):
                lo = g * HALF
                q = jnp.concatenate([ordered[rows, lo + k * HD : lo + (k + 1) * HD] for k in range(GROUP)], axis=0)
                at_k, at_v = FEAT + g * HD, FEAT + (KV + g) * HD
                new_k = [ordered[rows, at_k : at_k + HD], mothers[rows, g * HD : (g + 1) * HD]]
                new_v = [ordered[rows, at_v : at_v + HD], mothers[rows, (KV + g) * HD : (KV + g + 1) * HD]]
                base = 16 * len(jobs)
                also = jnp.logical_or(extra == slot + base, jnp.logical_and(extra == slot + base + 8, flag))
                jobs.append((h, g, rows, inside, also, q.astype(BF16), new_k, new_v))
        new_k = jnp.concatenate([v for job in jobs for v in job[6]]).astype(BF16)
        new_v = jnp.concatenate([v for job in jobs for v in job[7]]).astype(BF16)
        new_s = lax.dot_general(
            jnp.concatenate([job[5] for job in jobs]), new_k, last, preferred_element_type=F32
        )
        mixes, new_w, folded, rest = [], [], [], []
        for w, (h, g, rows, inside, also, q, _, _) in enumerate(jobs):
            scores = lax.dot_general(q, keys[h, g], last, preferred_element_type=F32)
            fresh = new_s[w * 8 * GROUP : (w + 1) * 8 * GROUP]
            scores = jnp.concatenate([jnp.where(inside, scores, NEG), jnp.where(also, fresh, NEG)], axis=1)
            top = jnp.max(scores, axis=-1, keepdims=True)
            weights = jnp.exp2(scores * scale - top * scale).astype(BF16)
            parts = [weights[:, n * 128 : (n + 1) * 128].astype(F32) for n in range(5)]
            total = ((parts[0] + parts[1]) + (parts[2] + parts[3])) + parts[4]
            folded.append(total.astype(BF16))
            rest.append((total - folded[-1].astype(F32)).astype(BF16))
            mixes.append(jnp.dot(weights[:, :CACHE], values[h, g], preferred_element_type=F32))
            new_w.append(weights[:, CACHE:])
        new_mix = jnp.dot(jnp.concatenate(new_w), new_v, preferred_element_type=F32)
        mass = jnp.dot(jnp.concatenate(folded), ones, preferred_element_type=F32)
        mass += jnp.dot(jnp.concatenate(rest), ones, preferred_element_type=F32)
        for w, (h, g, rows, _, _, _, _, _) in enumerate(jobs):
            mine = slice(w * 8 * GROUP, (w + 1) * 8 * GROUP)
            out = (mixes[w] + new_mix[mine]) / mass[mine]
            for k in range(GROUP):
                answer[g, rows, k * HD : (k + 1) * HD] = out[k * 8 : k * 8 + 8]
        return carry

    lax.fori_loop(0, (chunks[CHUNKS + 1] + 3) // 4, body, 0)
    which = [pl.ds(pl.multiple_of(lax.bitwise_xor(zi, zz) * FAMILY, FAMILY), FAMILY) for zz in range(2)]
    turn = jnp.concatenate([back[w, :] for w in which]).astype(BF16)
    for cc, outs in ((0, (keep0, keep1)), (1, (give0, give1))):
        feats = answer[lax.bitwise_xor(c, cc)].astype(BF16)
        both = jnp.dot(turn, feats, preferred_element_type=F32).astype(BF16)
        for zz, out in enumerate(outs):
            out[...] = both[zz * FAMILY : (zz + 1) * FAMILY]


def spread_kernel(a_ref, b_ref, c_ref, d_ref, out_ref):
    total = (a_ref[...] + b_ref[...]) + (c_ref[...] + d_ref[...])
    for z in range(8):
        out_ref[z] = total


def hold_kernel(*refs):
    pass


def half_rows(core):
    return pl.ds(pl.multiple_of(core * HALF, HALF), HALF)


def own_half_kernel(mine_ref, w0, w1, w2, w3, acc_ref):
    rows = half_rows(at("c"))
    for k, w in enumerate((w0, w1, w2, w3)):
        acc_ref[k] = jnp.dot(mine_ref[...], w[rows, :], preferred_element_type=F32)


def other_half_kernel(other_ref, acc_ref, w0, w1, w2, w3, o0, o1, o2, o3, blocks):
    c = at("c")
    rows = half_rows(1 - c)
    for k, w in enumerate((w0, w1, w2, w3)):
        total = acc_ref[k] + jnp.dot(other_ref[...], w[rows, :], preferred_element_type=F32)
        total = total.astype(BF16)
        where = jnp.where(c == 0, k, (4 - k) & 3)
        for zo in range(4):
            for zi in range(2):
                at_row = (zo * 2 + zi) * FAMILY
                blocks[where, zi, zo * FAMILY : (zo + 1) * FAMILY, :] = total[at_row : at_row + FAMILY]
    for s, out in enumerate((o0, o1, o2, o3)):
        out[...] = blocks[(at("y") - at("x") - s) & 3]


def permute(value, axes, move):
    sizes = [SIZES[AXES.index(a)] for a in axes]
    pairs = []
    for n in range(math.prod(sizes)):
        coords, rest = [], n
        for s in reversed(sizes):
            coords.append(rest % s)
            rest //= s
        flat = 0
        for t, s in zip(move(*reversed(coords)), sizes):
            flat = flat * s + t % s
        pairs.append((n, flat))
    return lax.ppermute(value, axes, pairs)


def swap_core(v):
    return permute(v, ("c",), lambda c: (1 - c,))


def swap_chip(v):
    return permute(v, ("zi",), lambda z: (1 - z,))


def swap_both(v):
    return permute(v, ("zi", "c"), lambda z, c: (1 - z, 1 - c))


def shape(*dims, dtype=BF16):
    return jax.ShapeDtypeStruct(dims, dtype)


def attend_call(*args):
    return pl.pallas_call(
        attend_kernel,
        out_shape=[shape(FAMILY, HALF)] * 4,
        in_specs=[VMEM, VMEM, SMEM] + [VMEM] * 6,
        out_specs=[VMEM] * 4,
        scratch_shapes=[
            pltpu.VMEM((ITEMS, WIDE), BF16),
            pltpu.VMEM((SLOTS, WIDE), F32),
            pltpu.VMEM((SLOTS, 2 * KV * HD), F32),
            pltpu.VMEM((KV, SLOTS, HALF), F32),
        ],
        compiler_params=LIMIT,
        cost_estimate=pl.CostEstimate(flops=70 * 10**8, bytes_accessed=10**6, transcendentals=0),
        name="attend",
    )(*args)


def per_device(queries, key_cache, value_cache, new_keys, new_values, lengths, ancestors, out_weight):
    m0 = jnp.concatenate([queries, new_keys, new_values], axis=-1).reshape(2 * HOLD, WIDE)
    m1 = swap_core(m0)
    m2 = swap_chip(m0)
    sort, back, chunks, keys, values, w0 = pl.pallas_call(
        plan_kernel,
        out_shape=[
            shape(SLOTS + 8, 128, dtype=F32),
            shape(ITEMS, 128, dtype=F32),
            shape(CHUNKS + 2 + HOLD, dtype=jnp.int32),
            pltpu.VMEM(key_cache.shape, BF16),
            pltpu.VMEM(value_cache.shape, BF16),
            pltpu.VMEM(out_weight.shape, BF16),
        ],
        in_specs=[HBM] * 5,
        out_specs=[VMEM, VMEM, SMEM, VMEM, VMEM, VMEM],
        scratch_shapes=[
            pltpu.SMEM(ancestors.shape, jnp.int32),
            pltpu.SMEM((HOLD,), jnp.int32),
            pltpu.SMEM((HOLD + 1,), jnp.int32),
            pltpu.SemaphoreType.DMA((5,)),
        ],
        compiler_params=LIMIT,
        cost_estimate=TINY,
        name="plan",
    )(*(pltpu.with_memory_space_constraint(v, pltpu.HBM) for v in (ancestors, lengths, key_cache, value_cache, out_weight)))
    def along(v):
        return permute(v, ("y", "c"), lambda y, c: (y + 1 + 2 * c, c))

    w_next = along(out_weight)
    w0_x = swap_core(out_weight)
    w_far = along(w_next)
    w_back = swap_core(along(w0_x))

    m2 = pl.pallas_call(
        hold_kernel,
        out_shape=shape(2 * HOLD, WIDE),
        in_specs=[VMEM] * 2,
        out_specs=VMEM,
        input_output_aliases={0: 0},
        compiler_params=LIMIT,
        cost_estimate=TINY,
        name="relay",
    )(m2, back)
    m3 = swap_core(m2)
    keep0, keep1, give0, give1 = attend_call(sort, back, chunks, m0, m1, m2, m3, keys, values)
    far = swap_both(give1)
    near = swap_chip(keep1)
    beside = swap_core(give0)
    spread = pl.pallas_call(
        spread_kernel,
        out_shape=shape(8, FAMILY, HALF),
        in_specs=[VMEM] * 4,
        out_specs=VMEM,
        compiler_params=pltpu.CompilerParams(vmem_limit_bytes=8 * 2**20),
        cost_estimate=pl.CostEstimate(flops=12 * 10**9, bytes_accessed=10**5, transcendentals=0),
        name="spread",
    )(keep0, far, near, beside)
    mine = lax.all_to_all(spread, Z, split_axis=0, concat_axis=0).reshape(8 * FAMILY, HALF)
    rows = 8 * FAMILY
    w_specs = [VMEM] * 4
    w = (w0, w_next, w_far, w_back)
    mine = pl.pallas_call(
        hold_kernel,
        out_shape=shape(8 * FAMILY, HALF),
        in_specs=[VMEM] * 3,
        out_specs=VMEM,
        input_output_aliases={0: 0},
        compiler_params=LIMIT,
        cost_estimate=TINY,
        name="hold",
    )(mine, w_far, w_back)
    other = swap_core(mine)
    acc = pl.pallas_call(
        own_half_kernel,
        out_shape=shape(4, rows, 128, dtype=F32),
        in_specs=[VMEM] + w_specs,
        out_specs=VMEM,
        compiler_params=LIMIT,
        cost_estimate=pl.CostEstimate(flops=10**9, bytes_accessed=10**6, transcendentals=0),
        name="own_half",
    )(mine, *w)
    parts = pl.pallas_call(
        other_half_kernel,
        out_shape=[shape(2, rows // 2, 128)] * 4,
        in_specs=[VMEM, VMEM] + w_specs,
        out_specs=[VMEM] * 4,
        scratch_shapes=[pltpu.VMEM((4, 2, rows // 2, 128), BF16)],
        compiler_params=LIMIT,
        cost_estimate=pl.CostEstimate(flops=10**9, bytes_accessed=10**6, transcendentals=0),
        name="other_half",
    )(other, acc, *w)
    total = 0.0
    for k in (2, 1, 3, 0):
        total = total + permute(parts[k], ("y", "x"), lambda y, x, k=k: (x + k, y)).astype(F32)
    return total.astype(BF16)


def solution(mesh):
    fine = Mesh(mesh.devices.reshape(SIZES), AXES)
    in_specs = (
        P(None, DP, "x"),
        P(DP, "x", None, None),
        P(DP, "x", None, None),
        P(None, DP, "x"),
        P(None, DP, "x"),
        P(DP),
        P(),
        P("x", DP),
    )
    return jax.shard_map(
        per_device, mesh=fine, in_specs=in_specs, out_specs=P(None, "x", DP), check_vma=False
    )
```

```python
import math

import jax
import jax.numpy as jnp
from jax import lax
from jax.experimental import pallas as pl
from jax.experimental.pallas import tpu as pltpu
from jax.sharding import Mesh
from jax.sharding import PartitionSpec as P

FAMILY = 32
AXES = ("y", "zo", "zi", "c", "x")
SIZES = (4, 4, 2, 2, 4)
DP = ("y", "zo", "zi", "c")
Z = ("zo", "zi")

HOLD = 8
ITEMS = 64
CHUNKS = 16
SLOTS = CHUNKS * 8
KV = 2
GROUP = 8
HD = 128
HALF = GROUP * HD
FEAT = KV * HALF
WIDE = FEAT + 2 * KV * HD
CACHE = 512
NEG = -1e30

HBM = pl.BlockSpec(memory_space=pltpu.HBM)
VMEM = pl.BlockSpec(memory_space=pltpu.VMEM)
SMEM = pl.BlockSpec(memory_space=pltpu.SMEM)
F32 = jnp.float32
BF16 = jnp.bfloat16
LIMIT = pltpu.CompilerParams(vmem_limit_bytes=16 * 2**20)
TINY = pl.CostEstimate(flops=10**6, bytes_accessed=10**5, transcendentals=0)


def at(axis):
    return lax.axis_index(axis)


def plan_kernel(
    ancestors, lengths, key_ref, value_ref,
    sort_ref, back_ref, chunk_ref, keys, values,
    anc_ref, len_ref, free, sems,
):
    loads = [
        pltpu.make_async_copy(src, dst, sems.at[k])
        for k, (src, dst) in enumerate(
            ((ancestors, anc_ref), (lengths, len_ref), (key_ref, keys), (value_ref, values))
        )
    ]
    for load in loads:
        load.start()
    first = (at("y") * 4 + at("zo")) * FAMILY
    own = at("zi") * 2 + at("c")
    sort_ref[...] = jnp.zeros_like(sort_ref)
    for j in range(CHUNKS + 2):
        chunk_ref[j] = 0
    for h in range(HOLD):
        free[h] = 0
    free[HOLD] = SLOTS + 1
    lane = lax.broadcasted_iota(jnp.int32, (1, 128), 1)
    used = jnp.int32(0)
    for load in loads[:2]:
        load.wait()
    for h in range(HOLD):
        chunk_ref[CHUNKS + 2 + h] = len_ref[h]
    for block in range(4):
        place = lax.bitwise_xor(own, block) * 8
        for r in range(2):
            for i in range(8):
                n = block * 16 + r * 8 + i
                row = lane == n
                source = first + place + i
                if r:
                    source = anc_ref[1, source]
                    mp = source - first
                    row = jnp.logical_or(row, lane == lax.bitwise_xor(mp >> 3, own) * 16 + (mp & 7) + ITEMS)
                root = anc_ref[0, source] - first
                here = (root >> 3) == own
                h = jnp.where(here, root & 7, HOLD)
                slot = free[h]
                opens = (slot & 7) == 0
                slot = jnp.where(opens, used * 8, slot)
                free[h] = slot + jnp.where(here, 1, 0)
                chunk_ref[jnp.where(opens, used, CHUNKS)] = h
                used = used + jnp.where(opens, 1, 0)
                sort_ref[pl.ds(slot, 1), :] = jnp.where(row, 1.0, 0.0)
                back_ref[pl.ds(r * FAMILY + place + i, 1), :] = jnp.where(lane == slot, 1.0, 0.0)
    chunk_ref[CHUNKS + 1] = used
    for load in loads[2:]:
        load.wait()


def attend_kernel(
    plan, back, chunks, m0, m1, m2, m3, keys, values,
    keep0, keep1, give0, give1,
    message, ordered, mothers, answer,
):
    scale = math.log2(math.e) / math.sqrt(HD)
    zi, c = at("zi"), at("c")
    for b, m in enumerate((m0, m1, m2, m3)):
        message[b * 16 : b * 16 + 16, :] = m[...]
    answer[...] = jnp.zeros_like(answer)
    sort = plan[0:SLOTS, 0:ITEMS].astype(BF16)
    ordered[...] = jnp.dot(sort, message[...], preferred_element_type=F32)
    pick = plan[0:SLOTS, ITEMS : 2 * ITEMS].astype(BF16)
    mothers[...] = jnp.dot(pick, message[:, FEAT:], preferred_element_type=F32)
    places = lax.broadcasted_iota(jnp.int32, (1, CACHE), 1)
    lane = lax.broadcasted_iota(jnp.int32, (8, 128), 1)
    slot = lax.broadcasted_iota(jnp.int32, (8 * GROUP, 128), 0) & 7
    extra = lax.broadcasted_iota(jnp.int32, (8 * GROUP, 128), 1)
    ones = jnp.ones((2 * HD, HD), BF16)
    last = (((1,), (1,)), ((), ()))

    def body(p, carry):
        jobs = []
        for u in range(4):
            j = 4 * p + u
            h = chunks[j]
            inside = places < chunks[CHUNKS + 2 + h]
            rows = pl.ds(pl.multiple_of(j * 8, 8), 8)
            has = jnp.sum(jnp.where(lane >= ITEMS, plan[rows, :], 0.0), axis=-1, keepdims=True)
            flag = jnp.concatenate([has] * GROUP, axis=0) > 0.5
            for g in range(KV):
                lo = g * HALF
                q = jnp.concatenate([ordered[rows, lo + k * HD : lo + (k + 1) * HD] for k in range(GROUP)], axis=0)
                at_k, at_v = FEAT + g * HD, FEAT + (KV + g) * HD
                new_k = [ordered[rows, at_k : at_k + HD], mothers[rows, g * HD : (g + 1) * HD]]
                new_v = [ordered[rows, at_v : at_v + HD], mothers[rows, (KV + g) * HD : (KV + g + 1) * HD]]
                base = 16 * len(jobs)
                also = jnp.logical_or(extra == slot + base, jnp.logical_and(extra == slot + base + 8, flag))
                jobs.append((h, g, rows, inside, also, q.astype(BF16), new_k, new_v))
        new_k = jnp.concatenate([v for job in jobs for v in job[6]]).astype(BF16)
        new_v = jnp.concatenate([v for job in jobs for v in job[7]]).astype(BF16)
        new_s = lax.dot_general(
            jnp.concatenate([job[5] for job in jobs]), new_k, last, preferred_element_type=F32
        )
        mixes, new_w, folded, rest = [], [], [], []
        for w, (h, g, rows, inside, also, q, _, _) in enumerate(jobs):
            scores = lax.dot_general(q, keys[h, g], last, preferred_element_type=F32)
            fresh = new_s[w * 8 * GROUP : (w + 1) * 8 * GROUP]
            scores = jnp.concatenate([jnp.where(inside, scores, NEG), jnp.where(also, fresh, NEG)], axis=1)
            top = jnp.max(scores, axis=-1, keepdims=True)
            weights = jnp.exp2(scores * scale - top * scale).astype(BF16)
            parts = [weights[:, n * 128 : (n + 1) * 128].astype(F32) for n in range(5)]
            total = ((parts[0] + parts[1]) + (parts[2] + parts[3])) + parts[4]
            folded.append(total.astype(BF16))
            rest.append((total - folded[-1].astype(F32)).astype(BF16))
            mixes.append(jnp.dot(weights[:, :CACHE], values[h, g], preferred_element_type=F32))
            new_w.append(weights[:, CACHE:])
        new_mix = jnp.dot(jnp.concatenate(new_w), new_v, preferred_element_type=F32)
        halves = jnp.concatenate([jnp.concatenate(folded), jnp.concatenate(rest)], axis=1)
        mass = jnp.dot(halves, ones, preferred_element_type=F32)
        for w, (h, g, rows, _, _, _, _, _) in enumerate(jobs):
            mine = slice(w * 8 * GROUP, (w + 1) * 8 * GROUP)
            out = (mixes[w] + new_mix[mine]) / mass[mine]
            for k in range(GROUP):
                answer[g, rows, k * HD : (k + 1) * HD] = out[k * 8 : k * 8 + 8]
        return carry

    lax.fori_loop(0, (chunks[CHUNKS + 1] + 3) // 4, body, 0)
    which = [pl.ds(pl.multiple_of(lax.bitwise_xor(zi, zz) * FAMILY, FAMILY), FAMILY) for zz in range(2)]
    turn = jnp.concatenate([back[w, :] for w in which]).astype(BF16)
    for cc, outs in ((0, (keep0, keep1)), (1, (give0, give1))):
        feats = answer[lax.bitwise_xor(c, cc)].astype(BF16)
        both = jnp.dot(turn, feats, preferred_element_type=F32).astype(BF16)
        for zz, out in enumerate(outs):
            out[...] = both[zz * FAMILY : (zz + 1) * FAMILY]


def bring_kernel(src, dst, sem):
    load = pltpu.make_async_copy(src, dst, sem)
    load.start()
    load.wait()


def spread_kernel(a_ref, b_ref, c_ref, d_ref, out_ref):
    total = (a_ref[...] + b_ref[...]) + (c_ref[...] + d_ref[...])
    for z in range(8):
        out_ref[z] = total


def hold_kernel(*refs):
    pass


def half_rows(core):
    return pl.ds(pl.multiple_of(core * HALF, HALF), HALF)


def own_half_kernel(mine_ref, w0, w1, w2, w3, acc_ref):
    rows = half_rows(at("c"))
    for k, w in enumerate((w0, w1, w2, w3)):
        acc_ref[k] = jnp.dot(mine_ref[...], w[rows, :], preferred_element_type=F32)


def other_half_kernel(other_ref, acc_ref, w0, w1, w2, w3, o0, o1, o2, o3, blocks):
    c = at("c")
    rows = half_rows(1 - c)
    for k, w in enumerate((w0, w1, w2, w3)):
        total = acc_ref[k] + jnp.dot(other_ref[...], w[rows, :], preferred_element_type=F32)
        total = total.astype(BF16)
        where = jnp.where(c == 0, k, (4 - k) & 3)
        for zo in range(4):
            for zi in range(2):
                at_row = (zo * 2 + zi) * FAMILY
                blocks[where, zi, zo * FAMILY : (zo + 1) * FAMILY, :] = total[at_row : at_row + FAMILY]
    for s, out in enumerate((o0, o1, o2, o3)):
        out[...] = blocks[(at("y") - at("x") - s) & 3]


def permute(value, axes, move):
    sizes = [SIZES[AXES.index(a)] for a in axes]
    pairs = []
    for n in range(math.prod(sizes)):
        coords, rest = [], n
        for s in reversed(sizes):
            coords.append(rest % s)
            rest //= s
        flat = 0
        for t, s in zip(move(*reversed(coords)), sizes):
            flat = flat * s + t % s
        pairs.append((n, flat))
    return lax.ppermute(value, axes, pairs)


def swap_core(v):
    return permute(v, ("c",), lambda c: (1 - c,))


def swap_chip(v):
    return permute(v, ("zi",), lambda z: (1 - z,))


def swap_both(v):
    return permute(v, ("zi", "c"), lambda z, c: (1 - z, 1 - c))


def shape(*dims, dtype=BF16):
    return jax.ShapeDtypeStruct(dims, dtype)


def attend_call(*args):
    return pl.pallas_call(
        attend_kernel,
        out_shape=[shape(FAMILY, HALF)] * 4,
        in_specs=[VMEM, VMEM, SMEM] + [VMEM] * 6,
        out_specs=[VMEM] * 4,
        scratch_shapes=[
            pltpu.VMEM((ITEMS, WIDE), BF16),
            pltpu.VMEM((SLOTS, WIDE), F32),
            pltpu.VMEM((SLOTS, 2 * KV * HD), F32),
            pltpu.VMEM((KV, SLOTS, HALF), F32),
        ],
        compiler_params=LIMIT,
        cost_estimate=pl.CostEstimate(flops=70 * 10**8, bytes_accessed=10**6, transcendentals=0),
        name="attend",
    )(*args)


def per_device(queries, key_cache, value_cache, new_keys, new_values, lengths, ancestors, out_weight):
    m0 = jnp.concatenate([queries, new_keys, new_values], axis=-1).reshape(2 * HOLD, WIDE)
    m1 = swap_core(m0)
    m2 = swap_chip(m0)
    sort, back, chunks, keys, values = pl.pallas_call(
        plan_kernel,
        out_shape=[
            shape(SLOTS + 8, 128, dtype=F32),
            shape(ITEMS, 128, dtype=F32),
            shape(CHUNKS + 2 + HOLD, dtype=jnp.int32),
            pltpu.VMEM(key_cache.shape, BF16),
            pltpu.VMEM(value_cache.shape, BF16),
        ],
        in_specs=[HBM] * 4,
        out_specs=[VMEM, VMEM, SMEM, VMEM, VMEM],
        scratch_shapes=[
            pltpu.SMEM(ancestors.shape, jnp.int32),
            pltpu.SMEM((HOLD,), jnp.int32),
            pltpu.SMEM((HOLD + 1,), jnp.int32),
            pltpu.SemaphoreType.DMA((4,)),
        ],
        compiler_params=LIMIT,
        cost_estimate=TINY,
        name="plan",
    )(*(pltpu.with_memory_space_constraint(v, pltpu.HBM) for v in (ancestors, lengths, key_cache, value_cache)))
    w0 = pl.pallas_call(
        bring_kernel,
        out_shape=pltpu.VMEM(out_weight.shape, BF16),
        in_specs=[HBM],
        out_specs=VMEM,
        scratch_shapes=[pltpu.SemaphoreType.DMA],
        compiler_params=LIMIT,
        cost_estimate=TINY,
        name="bring",
    )(pltpu.with_memory_space_constraint(out_weight, pltpu.HBM))
    def along(v):
        return permute(v, ("y", "c"), lambda y, c: (y + 1 + 2 * c, c))

    w_next = along(out_weight)
    w0_x = swap_core(out_weight)
    w_far = along(w_next)
    w_back = swap_core(along(w0_x))

    m2 = pl.pallas_call(
        hold_kernel,
        out_shape=shape(2 * HOLD, WIDE),
        in_specs=[VMEM] * 2,
        out_specs=VMEM,
        input_output_aliases={0: 0},
        compiler_params=LIMIT,
        cost_estimate=TINY,
        name="relay",
    )(m2, back)
    m3 = swap_core(m2)
    keep0, keep1, give0, give1 = attend_call(sort, back, chunks, m0, m1, m2, m3, keys, values)
    far = swap_both(give1)
    near = swap_chip(keep1)
    beside = swap_core(give0)
    spread = pl.pallas_call(
        spread_kernel,
        out_shape=shape(8, FAMILY, HALF),
        in_specs=[VMEM] * 4,
        out_specs=VMEM,
        compiler_params=pltpu.CompilerParams(vmem_limit_bytes=8 * 2**20),
        cost_estimate=pl.CostEstimate(flops=12 * 10**9, bytes_accessed=10**5, transcendentals=0),
        name="spread",
    )(keep0, far, near, beside)
    mine = lax.all_to_all(spread, Z, split_axis=0, concat_axis=0).reshape(8 * FAMILY, HALF)
    rows = 8 * FAMILY
    w_specs = [VMEM] * 4
    w = (w0, w_next, w_far, w_back)
    mine = pl.pallas_call(
        hold_kernel,
        out_shape=shape(8 * FAMILY, HALF),
        in_specs=[VMEM] * 4,
        out_specs=VMEM,
        input_output_aliases={0: 0},
        compiler_params=LIMIT,
        cost_estimate=TINY,
        name="hold",
    )(mine, w_far, w_back, w0)
    other = swap_core(mine)
    acc = pl.pallas_call(
        own_half_kernel,
        out_shape=shape(4, rows, 128, dtype=F32),
        in_specs=[VMEM] + w_specs,
        out_specs=VMEM,
        compiler_params=LIMIT,
        cost_estimate=pl.CostEstimate(flops=10**9, bytes_accessed=10**6, transcendentals=0),
        name="own_half",
    )(mine, *w)
    parts = pl.pallas_call(
        other_half_kernel,
        out_shape=[shape(2, rows // 2, 128)] * 4,
        in_specs=[VMEM, VMEM] + w_specs,
        out_specs=[VMEM] * 4,
        scratch_shapes=[pltpu.VMEM((4, 2, rows // 2, 128), BF16)],
        compiler_params=LIMIT,
        cost_estimate=pl.CostEstimate(flops=10**9, bytes_accessed=10**6, transcendentals=0),
        name="other_half",
    )(other, acc, *w)
    total = 0.0
    for k in (2, 1, 3, 0):
        total = total + permute(parts[k], ("y", "x"), lambda y, x, k=k: (x + k, y)).astype(F32)
    return total.astype(BF16)


def solution(mesh):
    fine = Mesh(mesh.devices.reshape(SIZES), AXES)
    in_specs = (
        P(None, DP, "x"),
        P(DP, "x", None, None),
        P(DP, "x", None, None),
        P(None, DP, "x"),
        P(None, DP, "x"),
        P(DP),
        P(),
        P("x", DP),
    )
    return jax.shard_map(
        per_device, mesh=fine, in_specs=in_specs, out_specs=P(None, "x", DP), check_vma=False
    )
```

```python
import math

import jax
import jax.numpy as jnp
from jax import lax
from jax.experimental import pallas as pl
from jax.experimental.pallas import tpu as pltpu
from jax.sharding import Mesh
from jax.sharding import PartitionSpec as P

FAMILY = 32
AXES = ("y", "zo", "zi", "c", "x")
SIZES = (4, 4, 2, 2, 4)
DP = ("y", "zo", "zi", "c")
Z = ("zo", "zi")

HOLD = 8
ITEMS = 64
CHUNKS = 16
SLOTS = CHUNKS * 8
KV = 2
GROUP = 8
HD = 128
HALF = GROUP * HD
FEAT = KV * HALF
WIDE = FEAT + 2 * KV * HD
CACHE = 512
NEG = -1e30

HBM = pl.BlockSpec(memory_space=pltpu.HBM)
VMEM = pl.BlockSpec(memory_space=pltpu.VMEM)
SMEM = pl.BlockSpec(memory_space=pltpu.SMEM)
F32 = jnp.float32
BF16 = jnp.bfloat16
LIMIT = pltpu.CompilerParams(vmem_limit_bytes=16 * 2**20)
TINY = pl.CostEstimate(flops=10**6, bytes_accessed=10**5, transcendentals=0)


def at(axis):
    return lax.axis_index(axis)


def plan_kernel(
    ancestors, lengths, key_ref, value_ref, w_ref,
    sort_ref, back_ref, chunk_ref, keys, values, w0,
    anc_ref, len_ref, free, sems,
):
    loads = [
        pltpu.make_async_copy(src, dst, sems.at[k])
        for k, (src, dst) in enumerate(
            ((ancestors, anc_ref), (lengths, len_ref), (key_ref, keys), (value_ref, values), (w_ref, w0))
        )
    ]
    for load in loads:
        load.start()
    first = (at("y") * 4 + at("zo")) * FAMILY
    own = at("zi") * 2 + at("c")
    sort_ref[...] = jnp.zeros_like(sort_ref)
    for j in range(CHUNKS + 2):
        chunk_ref[j] = 0
    for h in range(HOLD):
        free[h] = 0
    free[HOLD] = SLOTS + 1
    lane = lax.broadcasted_iota(jnp.int32, (1, 128), 1)
    used = jnp.int32(0)
    for load in loads[:2]:
        load.wait()
    for h in range(HOLD):
        chunk_ref[CHUNKS + 2 + h] = len_ref[h]
    for block in range(4):
        place = lax.bitwise_xor(own, block) * 8
        for r in range(2):
            for i in range(8):
                n = block * 16 + r * 8 + i
                row = lane == n
                source = first + place + i
                if r:
                    source = anc_ref[1, source]
                    mp = source - first
                    row = jnp.logical_or(row, lane == lax.bitwise_xor(mp >> 3, own) * 16 + (mp & 7) + ITEMS)
                root = anc_ref[0, source] - first
                here = (root >> 3) == own
                h = jnp.where(here, root & 7, HOLD)
                slot = free[h]
                opens = (slot & 7) == 0
                slot = jnp.where(opens, used * 8, slot)
                free[h] = slot + jnp.where(here, 1, 0)
                chunk_ref[jnp.where(opens, used, CHUNKS)] = h
                used = used + jnp.where(opens, 1, 0)
                sort_ref[pl.ds(slot, 1), :] = jnp.where(row, 1.0, 0.0)
                back_ref[pl.ds(r * FAMILY + place + i, 1), :] = jnp.where(lane == slot, 1.0, 0.0)
    chunk_ref[CHUNKS + 1] = used
    for load in loads[2:]:
        load.wait()


def attend_kernel(
    plan, back, chunks, m0, m1, m2, m3, keys, values,
    keep0, keep1, give0, give1,
    message, ordered, mothers, answer,
):
    scale = math.log2(math.e) / math.sqrt(HD)
    zi, c = at("zi"), at("c")
    for b, m in enumerate((m0, m1, m2, m3)):
        message[b * 16 : b * 16 + 16, :] = m[...]
    answer[...] = jnp.zeros_like(answer)
    sort = plan[0:SLOTS, 0:ITEMS].astype(BF16)
    ordered[...] = jnp.dot(sort, message[...], preferred_element_type=F32)
    pick = plan[0:SLOTS, ITEMS : 2 * ITEMS].astype(BF16)
    mothers[...] = jnp.dot(pick, message[:, FEAT:], preferred_element_type=F32)
    places = lax.broadcasted_iota(jnp.int32, (1, CACHE), 1)
    lane = lax.broadcasted_iota(jnp.int32, (8, 128), 1)
    slot = lax.broadcasted_iota(jnp.int32, (8 * GROUP, 128), 0) & 7
    extra = lax.broadcasted_iota(jnp.int32, (8 * GROUP, 128), 1)
    ones = jnp.ones((2 * HD, HD), BF16)
    last = (((1,), (1,)), ((), ()))

    def body(p, carry):
        jobs = []
        for u in range(4):
            j = 4 * p + u
            h = chunks[j]
            inside = places < chunks[CHUNKS + 2 + h]
            rows = pl.ds(pl.multiple_of(j * 8, 8), 8)
            has = jnp.sum(jnp.where(lane >= ITEMS, plan[rows, :], 0.0), axis=-1, keepdims=True)
            flag = jnp.concatenate([has] * GROUP, axis=0) > 0.5
            for g in range(KV):
                lo = g * HALF
                q = jnp.concatenate([ordered[rows, lo + k * HD : lo + (k + 1) * HD] for k in range(GROUP)], axis=0)
                at_k, at_v = FEAT + g * HD, FEAT + (KV + g) * HD
                new_k = [ordered[rows, at_k : at_k + HD], mothers[rows, g * HD : (g + 1) * HD]]
                new_v = [ordered[rows, at_v : at_v + HD], mothers[rows, (KV + g) * HD : (KV + g + 1) * HD]]
                base = 16 * len(jobs)
                also = jnp.logical_or(extra == slot + base, jnp.logical_and(extra == slot + base + 8, flag))
                jobs.append((h, g, rows, inside, also, q.astype(BF16), new_k, new_v))
        new_k = jnp.concatenate([v for job in jobs for v in job[6]]).astype(BF16)
        new_v = jnp.concatenate([v for job in jobs for v in job[7]]).astype(BF16)
        new_s = lax.dot_general(
            jnp.concatenate([job[5] for job in jobs]), new_k, last, preferred_element_type=F32
        )
        mixes, new_w, folded, rest = [], [], [], []
        for w, (h, g, rows, inside, also, q, _, _) in enumerate(jobs):
            scores = lax.dot_general(q, keys[h, g], last, preferred_element_type=F32)
            fresh = new_s[w * 8 * GROUP : (w + 1) * 8 * GROUP]
            scores = jnp.concatenate([jnp.where(inside, scores, NEG), jnp.where(also, fresh, NEG)], axis=1)
            top = jnp.max(scores, axis=-1, keepdims=True)
            weights = jnp.exp2(scores * scale - top * scale).astype(BF16)
            parts = [weights[:, n * 128 : (n + 1) * 128].astype(F32) for n in range(5)]
            total = ((parts[0] + parts[1]) + (parts[2] + parts[3])) + parts[4]
            folded.append(total.astype(BF16))
            rest.append((total - folded[-1].astype(F32)).astype(BF16))
            mixes.append(jnp.dot(weights[:, :CACHE], values[h, g], preferred_element_type=F32))
            new_w.append(weights[:, CACHE:])
        new_mix = jnp.dot(jnp.concatenate(new_w), new_v, preferred_element_type=F32)
        halves = jnp.concatenate([jnp.concatenate(folded), jnp.concatenate(rest)], axis=1)
        mass = jnp.dot(halves, ones, preferred_element_type=F32)
        for w, (h, g, rows, _, _, _, _, _) in enumerate(jobs):
            mine = slice(w * 8 * GROUP, (w + 1) * 8 * GROUP)
            out = (mixes[w] + new_mix[mine]) / mass[mine]
            for k in range(GROUP):
                answer[g, rows, k * HD : (k + 1) * HD] = out[k * 8 : k * 8 + 8]
        return carry

    lax.fori_loop(0, (chunks[CHUNKS + 1] + 3) // 4, body, 0)
    which = [pl.ds(pl.multiple_of(lax.bitwise_xor(zi, zz) * FAMILY, FAMILY), FAMILY) for zz in range(2)]
    turn = jnp.concatenate([back[w, :] for w in which]).astype(BF16)
    for cc, outs in ((0, (keep0, keep1)), (1, (give0, give1))):
        feats = answer[lax.bitwise_xor(c, cc)].astype(BF16)
        both = jnp.dot(turn, feats, preferred_element_type=F32).astype(BF16)
        for zz, out in enumerate(outs):
            out[...] = both[zz * FAMILY : (zz + 1) * FAMILY]


def spread_kernel(a_ref, b_ref, c_ref, d_ref, out_ref):
    total = (a_ref[...] + b_ref[...]) + (c_ref[...] + d_ref[...])
    for z in range(8):
        out_ref[z] = total


def hold_kernel(*refs):
    pass


def half_rows(core):
    return pl.ds(pl.multiple_of(core * HALF, HALF), HALF)


def own_half_kernel(mine_ref, w0, w1, w2, w3, acc_ref):
    rows = half_rows(at("c"))
    for k, w in enumerate((w0, w1, w2, w3)):
        acc_ref[k] = jnp.dot(mine_ref[...], w[rows, :], preferred_element_type=F32)


def other_half_kernel(other_ref, acc_ref, w0, w1, w2, w3, o0, o1, o2, o3, blocks):
    c = at("c")
    rows = half_rows(1 - c)
    for k, w in enumerate((w0, w1, w2, w3)):
        total = acc_ref[k] + jnp.dot(other_ref[...], w[rows, :], preferred_element_type=F32)
        total = total.astype(BF16)
        where = jnp.where(c == 0, k, (4 - k) & 3)
        for zo in range(4):
            for zi in range(2):
                at_row = (zo * 2 + zi) * FAMILY
                blocks[where, zi, zo * FAMILY : (zo + 1) * FAMILY, :] = total[at_row : at_row + FAMILY]
    for s, out in enumerate((o0, o1, o2, o3)):
        out[...] = blocks[(at("y") - at("x") - s) & 3]


def permute(value, axes, move):
    sizes = [SIZES[AXES.index(a)] for a in axes]
    pairs = []
    for n in range(math.prod(sizes)):
        coords, rest = [], n
        for s in reversed(sizes):
            coords.append(rest % s)
            rest //= s
        flat = 0
        for t, s in zip(move(*reversed(coords)), sizes):
            flat = flat * s + t % s
        pairs.append((n, flat))
    return lax.ppermute(value, axes, pairs)


def swap_core(v):
    return permute(v, ("c",), lambda c: (1 - c,))


def swap_chip(v):
    return permute(v, ("zi",), lambda z: (1 - z,))


def swap_both(v):
    return permute(v, ("zi", "c"), lambda z, c: (1 - z, 1 - c))


def shape(*dims, dtype=BF16):
    return jax.ShapeDtypeStruct(dims, dtype)


def attend_call(*args):
    return pl.pallas_call(
        attend_kernel,
        out_shape=[shape(FAMILY, HALF)] * 4,
        in_specs=[VMEM, VMEM, SMEM] + [VMEM] * 6,
        out_specs=[VMEM] * 4,
        scratch_shapes=[
            pltpu.VMEM((ITEMS, WIDE), BF16),
            pltpu.VMEM((SLOTS, WIDE), F32),
            pltpu.VMEM((SLOTS, 2 * KV * HD), F32),
            pltpu.VMEM((KV, SLOTS, HALF), F32),
        ],
        compiler_params=LIMIT,
        cost_estimate=pl.CostEstimate(flops=70 * 10**8, bytes_accessed=10**6, transcendentals=0),
        name="attend",
    )(*args)


def per_device(queries, key_cache, value_cache, new_keys, new_values, lengths, ancestors, out_weight):
    m0 = jnp.concatenate([queries, new_keys, new_values], axis=-1).reshape(2 * HOLD, WIDE)
    m1 = swap_core(m0)
    m2 = swap_chip(m0)
    sort, back, chunks, keys, values, w0 = pl.pallas_call(
        plan_kernel,
        out_shape=[
            shape(SLOTS + 8, 128, dtype=F32),
            shape(ITEMS, 128, dtype=F32),
            shape(CHUNKS + 2 + HOLD, dtype=jnp.int32),
            pltpu.VMEM(key_cache.shape, BF16),
            pltpu.VMEM(value_cache.shape, BF16),
            pltpu.VMEM(out_weight.shape, BF16),
        ],
        in_specs=[HBM] * 5,
        out_specs=[VMEM, VMEM, SMEM, VMEM, VMEM, VMEM],
        scratch_shapes=[
            pltpu.SMEM(ancestors.shape, jnp.int32),
            pltpu.SMEM((HOLD,), jnp.int32),
            pltpu.SMEM((HOLD + 1,), jnp.int32),
            pltpu.SemaphoreType.DMA((5,)),
        ],
        compiler_params=LIMIT,
        cost_estimate=TINY,
        name="plan",
    )(*(pltpu.with_memory_space_constraint(v, pltpu.HBM) for v in (ancestors, lengths, key_cache, value_cache, out_weight)))
    def along(v):
        return permute(v, ("y", "c"), lambda y, c: (y + 1 + 2 * c, c))

    w_next = along(out_weight)
    w0_x = swap_core(out_weight)
    w_far = along(w_next)
    w_back = swap_core(along(w0_x))

    m2 = pl.pallas_call(
        hold_kernel,
        out_shape=shape(2 * HOLD, WIDE),
        in_specs=[VMEM] * 2,
        out_specs=VMEM,
        input_output_aliases={0: 0},
        compiler_params=LIMIT,
        cost_estimate=TINY,
        name="relay",
    )(m2, back)
    m3 = swap_core(m2)
    keep0, keep1, give0, give1 = attend_call(sort, back, chunks, m0, m1, m2, m3, keys, values)
    far = swap_both(give1)
    near = swap_chip(keep1)
    beside = swap_core(give0)
    spread = pl.pallas_call(
        spread_kernel,
        out_shape=shape(8, FAMILY, HALF),
        in_specs=[VMEM] * 4,
        out_specs=VMEM,
        compiler_params=pltpu.CompilerParams(vmem_limit_bytes=8 * 2**20),
        cost_estimate=pl.CostEstimate(flops=12 * 10**9, bytes_accessed=10**5, transcendentals=0),
        name="spread",
    )(keep0, far, near, beside)
    mine = lax.all_to_all(spread, Z, split_axis=0, concat_axis=0).reshape(8 * FAMILY, HALF)
    rows = 8 * FAMILY
    w_specs = [VMEM] * 4
    w = (w0, w_next, w_far, w_back)
    mine = pl.pallas_call(
        hold_kernel,
        out_shape=shape(8 * FAMILY, HALF),
        in_specs=[VMEM] * 3,
        out_specs=VMEM,
        input_output_aliases={0: 0},
        compiler_params=LIMIT,
        cost_estimate=TINY,
        name="hold",
    )(mine, w_far, w_back)
    other = swap_core(mine)
    acc = pl.pallas_call(
        own_half_kernel,
        out_shape=shape(4, rows, 128, dtype=F32),
        in_specs=[VMEM] + w_specs,
        out_specs=VMEM,
        compiler_params=LIMIT,
        cost_estimate=pl.CostEstimate(flops=10**9, bytes_accessed=10**6, transcendentals=0),
        name="own_half",
    )(mine, *w)
    parts = pl.pallas_call(
        other_half_kernel,
        out_shape=[shape(2, rows // 2, 128)] * 4,
        in_specs=[VMEM, VMEM] + w_specs,
        out_specs=[VMEM] * 4,
        scratch_shapes=[pltpu.VMEM((4, 2, rows // 2, 128), BF16)],
        compiler_params=LIMIT,
        cost_estimate=pl.CostEstimate(flops=10**9, bytes_accessed=10**6, transcendentals=0),
        name="other_half",
    )(other, acc, *w)
    total = 0.0
    for k in (2, 1, 3, 0):
        total = total + permute(parts[k], ("y", "x"), lambda y, x, k=k: (x + k, y)).astype(F32)
    return total.astype(BF16)


def solution(mesh):
    fine = Mesh(mesh.devices.reshape(SIZES), AXES)
    in_specs = (
        P(None, DP, "x"),
        P(DP, "x", None, None),
        P(DP, "x", None, None),
        P(None, DP, "x"),
        P(None, DP, "x"),
        P(DP),
        P(),
        P("x", DP),
    )
    return jax.shard_map(
        per_device, mesh=fine, in_specs=in_specs, out_specs=P(None, "x", DP), check_vma=False
    )
```
